256 devices in a mesh: ctx: 64 (over z, y_lo, x), head: 4 (over y_hi, core).
Axes of the slice: x: 4, y: 4 (y_hi: 2, y_lo: 2; y = y_hi * 2 + y_lo), z: 8, core: 2. Of those that a mesh axis runs over, the one named last changes fastest.
Arguments:
- query: bfloat16 [32768, 1024], P('ctx', 'head'), may hold values from -8 to 8
- key: bfloat16 [32768, 1024], P('ctx', 'head'), may hold values from -8 to 8
- value: bfloat16 [32768, 1024], P('ctx', 'head'), may hold values from -6 to 6
- pos_store: bfloat16 [2048, 1024], P('ctx', 'head'), may hold values from -6 to 6
- owner: int32 [64], replicated, may hold values from 0 to 63, each once
- block_mask: int32 [64, 4], P('ctx'), may hold values from 0 to 1, as said below
- content_bias: float32 [1024], P('head'), may hold values from -3 to 3
- pos_bias: float32 [1024], P('head'), may hold values from -3 to 3
- out_weight: bfloat16 [1024, 1024], P('head'), may hold values from -0.1875 to 0.1875
- d_layer: bfloat16 [32768, 1024], P('ctx', 'head'), may hold values from -6 to 6
Outputs:
- grad_query: bfloat16 [32768, 1024], P('ctx', 'head')
- grad_key: bfloat16 [32768, 1024], P('ctx', 'head')
- grad_value: bfloat16 [32768, 1024], P('ctx', 'head')
- grad_pos: bfloat16 [2048, 1024], P('ctx', 'head')
- grad_out_weight: bfloat16 [1024, 1024], P('head', 'ctx')
The draws below stay inside these ranges and needn't reach their ends.
Inputs may be any that keep to these rules, and one draw needn't show every extreme that they name: block_mask[c, 0] is 1 for every block c. `owner`: each of the 64 slots is named once.
All inputs are finite; a program needn't handle non-finite values.
Results may differ from the reference program's by a relative error of at most 0.013.
The reference program's roundings to bfloat16 on the way count: a program that leaves them out, or rounds other values in their place, can miss the bound.
Values may be sent and summed in bfloat16 or wider, within the bound.
No kernel may reach another device: no remote copies, remote signals or barrier semaphores. Data moves between devices by JAX's collectives and lax.ppermute only.
A program may use at most 128 MiB of HBM per device.

```python
import math
from functools import reduce
import jax
import jax.numpy as jnp
from jax import lax

HEADS = 16
HD = 64
W = 4
TOK_DEV = 512
DM = 1024
TOKENS = 32768
NDB = 64
REL = 2048
RB = 32


def draw_query(key, part):
    key = jax.random.fold_in(key, 11)
    values = jnp.clip(jax.random.normal(key, (TOKENS, HEADS * HD), jnp.float32), -6.0, 6.0)
    return values.astype(jnp.bfloat16)


def draw_key(key, part):
    key = jax.random.fold_in(key, 12)
    values = jnp.clip(jax.random.normal(key, (TOKENS, HEADS * HD), jnp.float32), -6.0, 6.0)
    return values.astype(jnp.bfloat16)


def draw_block_mask(key, part):
    key = jax.random.fold_in(key, 13)
    picks = jax.random.randint(key, (NDB, W), 0, 4)
    flags = jnp.where(picks > 0, 1, 0).astype(jnp.int32)
    return flags.at[:, 0].set(1)


def block_scale(key, dims, split, least, top_value):
    gain, own = 1.0, jax.random.fold_in(key, 6)
    for axis_at, parts in split:
        steps = jnp.exp(jax.random.uniform(jax.random.fold_in(own, axis_at), (parts,), jnp.float32, least / len(split), top_value / len(split)))
        gain = gain * jnp.repeat(steps, dims[axis_at] // parts).reshape([-1 if axis == axis_at else 1 for axis in range(len(dims))])
    return gain


def scatter_about(stream_key, shape, width, reach, pieces=(), kind=jnp.bfloat16):
    drawn = jax.random.normal(stream_key, shape, jnp.float32) * width
    if len(pieces) > 0:
        drawn = block_scale(stream_key, shape, pieces, -0.22, 0.18) * drawn
    return jnp.clip(drawn, min=-reach, max=reach).astype(kind)


def setup_inputs(seed: int = 0) -> dict:
    splits = jax.random.split(jax.random.key(seed), 11)
    return {
        "query": draw_query(jax.random.fold_in(splits[10], 71), 0),
        "key": draw_key(jax.random.fold_in(splits[10], 71), 0),
        "value": scatter_about(splits[2], (TOKENS, DM), 1.0, 6.0, ((0, 64), (1, 4))),
        "pos_store": scatter_about(splits[3], (REL, DM), 1.0, 6.0, ((0, 64), (1, 4))),
        "owner": jax.random.permutation(splits[4], NDB).astype(jnp.int32),
        "block_mask": draw_block_mask(jax.random.fold_in(splits[10], 71), 0),
        "content_bias": scatter_about(splits[6], (DM,), 0.5, 3.0, ((0, 4),), jnp.float32),
        "pos_bias": scatter_about(splits[7], (DM,), 0.5, 3.0, ((0, 4),), jnp.float32),
        "out_weight": scatter_about(splits[8], (DM, DM), DM ** -0.5, 0.1875, ((0, 4),)),
        "d_layer": scatter_about(splits[9], (TOKENS, DM), 1.0, 6.0, ((0, 64), (1, 4))),
    }


def product(spec, first_arg, second_arg):
    return jnp.einsum(spec, first_arg.astype(jnp.float32), second_arg.astype(jnp.float32))

def relative_shift(wide_scores):
    length = wide_scores.shape[0]
    flipped = wide_scores[:, ::-1].reshape(2 * length * length)
    kept = flipped[length - 1:length - 1 + length * (2 * length - 1)]
    return kept.reshape(length, 2 * length - 1)[:, :length]

def relative_unshift(narrow):
    length = narrow.shape[0]
    padded = jnp.pad(narrow, ((0, 0), (0, length - 1))).reshape(length * (2 * length - 1))
    padded = jnp.pad(padded, (length - 1, 1))
    return padded.reshape(length, 2 * length)[:, ::-1]

def head_backward(content_query, position_query, keys_window, values_window, pos_window, grad_attn, allowed):
    rows_here = content_query.shape[0]
    window = keys_window.shape[0]
    score_scale = 1.0 / math.sqrt(content_query.shape[1])
    scores = []
    for lag_index in range(window):
        content = product('ae,be->ab', content_query, keys_window[lag_index])
        pos_rows = pos_window[lag_index * rows_here:(lag_index + 2) * rows_here]
        wide_scores = product('ae,te->at', position_query, pos_rows)
        raw_scores = score_scale * (content + relative_shift(wide_scores))
        scores.append(jnp.where(allowed[lag_index], raw_scores, -jnp.inf))
    row_max = reduce(jnp.maximum, [lax.optimization_barrier(jnp.max(entry, axis=1, keepdims=True)) for entry in scores])
    weights = [jnp.exp(entry - row_max) for entry in scores]
    row_total = reduce(jnp.add, [lax.optimization_barrier(jnp.sum(entry, axis=1, keepdims=True)) for entry in weights])
    probs = [entry / row_total for entry in weights]
    probs_low = [entry.astype(jnp.bfloat16) for entry in probs]
    attention = reduce(jnp.add, [product('ab,be->ae', probs_low[lag_index], values_window[lag_index]) for lag_index in range(window)])
    attention = attention.astype(jnp.bfloat16)
    row_dot = lax.optimization_barrier(jnp.sum(grad_attn.astype(jnp.float32) * attention.astype(jnp.float32), axis=1, keepdims=True))
    grad_content = jnp.zeros(content_query.shape, jnp.float32)
    grad_position = jnp.zeros(content_query.shape, jnp.float32)
    grad_window = jnp.zeros(pos_window.shape, jnp.float32)
    grad_keys = []
    grad_values = []
    for lag_index in range(window):
        grad_probs = product('ae,be->ab', grad_attn, values_window[lag_index])
        dscore = (score_scale * probs[lag_index] * (grad_probs - row_dot)).astype(jnp.bfloat16)
        grad_values.append(product('ab,ae->be', probs_low[lag_index], grad_attn))
        grad_keys.append(product('ab,ae->be', dscore, content_query))
        grad_content = grad_content + product('ab,be->ae', dscore, keys_window[lag_index])
        spread = relative_unshift(dscore)
        pos_rows = pos_window[lag_index * rows_here:(lag_index + 2) * rows_here]
        grad_position = grad_position + product('at,te->ae', spread, pos_rows)
        grad_window = grad_window.at[lag_index * rows_here:(lag_index + 2) * rows_here].add(product('at,ae->te', spread, position_query))
    grad_query = (grad_content + grad_position).astype(jnp.bfloat16)
    return (attention, grad_query, jnp.stack(grad_keys), jnp.stack(grad_values), grad_window)

def reference(query, key, value, pos_store, owner, block_mask, content_bias, pos_bias, out_weight, d_layer):
    features = HEADS * HD
    dist_order = pos_store.reshape(NDB, RB, features)[owner].reshape(REL, features)
    pos_ext = jnp.concatenate([jnp.zeros((TOK_DEV, features), jnp.bfloat16), dist_order], 0)
    pos_heads = pos_ext.reshape(-1, HEADS, HD).transpose(1, 0, 2)
    content_all = (query.astype(jnp.float32) + content_bias).astype(jnp.bfloat16)
    position_all = (query.astype(jnp.float32) + pos_bias).astype(jnp.bfloat16)
    grad_attn_all = jnp.dot(d_layer, out_weight.T, preferred_element_type=jnp.float32).astype(jnp.bfloat16)
    row_ids = jnp.arange(TOK_DEV, dtype=jnp.int32)
    causal_mask = row_ids[None, :] <= row_ids[:, None]

    def to_heads(matrix):
        return matrix.reshape(matrix.shape[0], HEADS, HD).transpose(1, 0, 2)

    def rows_of(matrix, first_row):
        return lax.dynamic_slice_in_dim(matrix, first_row, TOK_DEV, 0)

    def one_block(running, block_index):
        grad_key_all, grad_value_all, grad_window_all, grad_weight = running
        row_start = block_index * TOK_DEV
        starts = [jnp.maximum(block_index - lag_index, 0) * TOK_DEV for lag_index in range(W)]
        keys_window = jnp.stack([rows_of(key, first_row) for first_row in starts])
        values_window = jnp.stack([rows_of(value, first_row) for first_row in starts])
        masks = []
        for lag_index in range(W):
            flag = (block_mask[block_index, lag_index] == 1) & (block_index - lag_index >= 0)
            if lag_index == 0:
                masks.append(jnp.logical_and(flag, causal_mask))
            else:
                masks.append(jnp.broadcast_to(flag, (TOK_DEV, TOK_DEV)))
        allowed = jnp.stack(masks)
        keys_heads = keys_window.reshape(W, TOK_DEV, HEADS, HD).transpose(2, 0, 1, 3)
        values_heads = values_window.reshape(W, TOK_DEV, HEADS, HD).transpose(2, 0, 1, 3)
        results = jax.vmap(head_backward, in_axes=(0, 0, 0, 0, 0, 0, None))(to_heads(rows_of(content_all, row_start)), to_heads(rows_of(position_all, row_start)), keys_heads, values_heads, pos_heads, to_heads(rows_of(grad_attn_all, row_start)), allowed)
        attention_heads, grad_query_heads, grad_keys_heads, grad_values_heads, grad_window_heads = results
        attention = attention_heads.transpose(1, 0, 2).reshape(TOK_DEV, features)
        key_terms = grad_keys_heads.transpose(1, 2, 0, 3).reshape(W, TOK_DEV, features)
        value_terms = grad_values_heads.transpose(1, 2, 0, 3).reshape(W, TOK_DEV, features)
        for lag_index in range(W):
            grad_key_all = lax.dynamic_update_slice_in_dim(grad_key_all, rows_of(grad_key_all, starts[lag_index]) + key_terms[lag_index], starts[lag_index], 0)
            grad_value_all = lax.dynamic_update_slice_in_dim(grad_value_all, rows_of(grad_value_all, starts[lag_index]) + value_terms[lag_index], starts[lag_index], 0)
        grad_window_all = grad_window_all + grad_window_heads.transpose(1, 0, 2).reshape(-1, features)
        grad_weight = grad_weight + jnp.dot(attention.T, rows_of(d_layer, row_start), preferred_element_type=jnp.float32)
        grad_query_rows = grad_query_heads.transpose(1, 0, 2).reshape(TOK_DEV, features)
        return ((grad_key_all, grad_value_all, grad_window_all, grad_weight), grad_query_rows)
    initial = (jnp.zeros((TOKENS, features), jnp.float32), jnp.zeros((TOKENS, features), jnp.float32), jnp.zeros(((W + 1) * TOK_DEV, features), jnp.float32), jnp.zeros((features, features), jnp.float32))
    running, grad_query_blocks = lax.scan(one_block, initial, jnp.arange(NDB, dtype=jnp.int32))
    grad_key_all, grad_value_all, grad_window_all, grad_weight = running
    grad_query = grad_query_blocks.reshape(TOKENS, features)
    dist_grad = grad_window_all[TOK_DEV:]
    inverse = jnp.argsort(owner)
    grad_pos = dist_grad.reshape(NDB, RB, features)[inverse].reshape(REL, features).astype(jnp.bfloat16)
    return (grad_query, grad_key_all.astype(jnp.bfloat16), grad_value_all.astype(jnp.bfloat16), grad_pos, grad_weight.astype(jnp.bfloat16))
```

```python
import functools
import jax
import jax.numpy as jnp
from jax import lax
from jax.experimental import pallas as pl
from jax.experimental.pallas import tpu as pltpu
from jax.sharding import PartitionSpec as P

HD = 64
NEG = -1e30


def nt(a, b):
    return lax.dot_general(a, b, (((1,), (1,)), ((), ())), preferred_element_type=jnp.float32)


def nn(a, b):
    return lax.dot_general(a, b, (((1,), (0,)), ((), ())), preferred_element_type=jnp.float32)


def tn(a, b):
    return lax.dot_general(a, b, (((0,), (0,)), ((), ())), preferred_element_type=jnp.float32)


def pair_kernel(
    owner_ref, flag_ref, q_ref, kv0, kv1, kv2, kv3, slots_ref, cb_ref, pb_ref, ga_ref,
    dq_ref, own_ref, far_ref, dpos_ref, att_ref,
    table, flipped, dkt, dvt, dpt,
):
    tokens = q_ref.shape[0]
    window = 4
    span = tokens * window
    half = tokens // 2
    wide = span + half
    slot_count = owner_ref.shape[0]
    slot_rows = slots_ref.shape[0] // slot_count
    keys = [kv.at[0] for kv in (kv3, kv2, kv1, kv0)]
    values = [kv.at[1] for kv in (kv3, kv2, kv1, kv0)]
    bf = jnp.bfloat16
    anti = (
        lax.broadcasted_iota(jnp.int32, (half, half), 0)
        + lax.broadcasted_iota(jnp.int32, (half, half), 1)
        == half - 1
    ).astype(jnp.float32).astype(bf)

    table[0:tokens, :] = jnp.zeros((tokens, 128), bf)
    for d in range(slot_count):
        at = pl.multiple_of(owner_ref[d] * slot_rows, slot_rows)
        table[tokens + d * slot_rows : tokens + (d + 1) * slot_rows, :] = slots_ref[pl.ds(at, slot_rows), :]
    count = (tokens + span) // half
    for i in range(count):
        flipped[(count - 1 - i) * half : (count - i) * half, :] = nn(
            anti, table[i * half : (i + 1) * half, :]
        ).astype(bf)
    dkt[...] = jnp.zeros_like(dkt)
    dvt[...] = jnp.zeros_like(dvt)
    dpt[...] = jnp.zeros_like(dpt)

    lane = lax.broadcasted_iota(jnp.int32, (1, 128), 1)
    for r in range(2):
        rows = slice(r * half, (r + 1) * half)
        query = q_ref[rows, :].astype(jnp.float32)
        cq = (query + cb_ref[...]).astype(bf)
        pq = (query + pb_ref[...]).astype(bf)
        ga = ga_ref[rows, :]
        att_both = []
        dq_both = []
        for h in range(2):
            mine = (lane // HD) == h
            cqm = jnp.where(mine, cq, jnp.zeros_like(cq))
            pqm = jnp.where(mine, pq, jnp.zeros_like(pq))
            gam = jnp.where(mine, ga, jnp.zeros_like(ga))
            cqs = cqm * jnp.asarray(0.125, bf)
            pqs = pqm * jnp.asarray(0.125, bf)
            base = half * (1 - r)
            rel = nt(pqs, flipped[base : base + wide, :])
            rel = pltpu.roll(rel, span + 1, 1, stride=1, stride_axis=0)
            scores = []
            for w in range(window):
                s = nt(cqs, keys[w][...]) + rel[:, w * tokens : (w + 1) * tokens]
                if w == window - 1:
                    row = lax.broadcasted_iota(jnp.int32, (half, tokens), 0) + r * half
                    col = lax.broadcasted_iota(jnp.int32, (half, tokens), 1)
                    s = jnp.where(col <= row, s, NEG)
                else:
                    s = jnp.where(flag_ref[window - 1 - w] == 1, s, NEG)
                scores.append(s)
            top = functools.reduce(jnp.maximum, [jnp.max(s, axis=1, keepdims=True) for s in scores])
            weights = [jnp.exp(s - top) for s in scores]
            total = functools.reduce(jnp.add, [jnp.sum(e, axis=1, keepdims=True) for e in weights])
            inv = 1.0 / total
            probs = [e * inv for e in weights]
            low = [p.astype(bf) for p in probs]
            att = functools.reduce(jnp.add, [nn(low[w], values[w][...]) for w in range(window)])
            att = jnp.where(mine, att, 0.0).astype(bf)
            att_both.append(att)
            dot = jnp.sum(gam.astype(jnp.float32) * att.astype(jnp.float32), axis=1, keepdims=True)
            flips = [None] * 8
            acc = None
            for w in range(window):
                cols = slice(w * tokens, (w + 1) * tokens)
                dp = nt(gam, values[w][...])
                ds = (0.125 * probs[w] * (dp - dot)).astype(bf)
                dvt[:, cols] += tn(gam, low[w])
                dkt[:, cols] += tn(cqm, ds)
                part = nn(ds, keys[w][...])
                acc = part if acc is None else acc + part
                for x in range(2):
                    flips[7 - (2 * w + x)] = nn(ds[:, x * half : (x + 1) * half], anti)
            spread = jnp.concatenate(flips + [jnp.zeros((half, half), jnp.float32)], axis=1)
            spread = pltpu.roll(spread, 1, 1, stride=1, stride_axis=0).astype(bf)
            start = half * r
            acc = acc + nn(spread, table[start : start + wide, :])
            dpt[:, start : start + wide] += tn(pqm, spread)
            dq_both.append(acc)
        att_ref[rows, :] = jnp.where(lane < HD, att_both[0], att_both[1])
        dq_ref[rows, :] = jnp.where(lane < HD, dq_both[0], dq_both[1]).astype(bf)
    for i, grad in enumerate((dkt, dvt)):
        for w in range(window):
            block = grad[:, w * tokens : (w + 1) * tokens].T
            if w == window - 1:
                own_ref[i] = block
            else:
                far_ref[window - 2 - w, i] = block.astype(bf)
    dist = dpt[:, tokens:].T.astype(bf)
    for d in range(slot_count):
        at = pl.multiple_of(owner_ref[d] * slot_rows, slot_rows)
        dpos_ref[pl.ds(at, slot_rows), :] = dist[d * slot_rows : (d + 1) * slot_rows, :]


def pair_call(owner, flags, q, kvs, slots, cb, pb, ga):
    tokens, features = q.shape
    pairs = features // 128
    rel = slots.shape[0]

    def col(rows):
        return pl.BlockSpec((rows, 128), lambda p, *_: (0, p))

    both = pl.BlockSpec((2, tokens, 128), lambda p, *_: (0, 0, p))
    bf = jnp.bfloat16
    return pl.pallas_call(
        pair_kernel,
        grid_spec=pltpu.PrefetchScalarGridSpec(
            num_scalar_prefetch=2,
            grid=(pairs,),
            in_specs=[col(tokens)] + [both] * 4 + [col(rel), col(1), col(1), col(tokens)],
            out_specs=[
                col(tokens),
                both,
                pl.BlockSpec((3, 2, tokens, 128), lambda p, *_: (0, 0, 0, p)),
                col(rel),
                col(tokens),
            ],
            scratch_shapes=[
                pltpu.VMEM((tokens + rel, 128), bf),
                pltpu.VMEM((tokens + rel, 128), bf),
                pltpu.VMEM((128, rel), jnp.float32),
                pltpu.VMEM((128, rel), jnp.float32),
                pltpu.VMEM((128, tokens + rel), jnp.float32),
            ],
        ),
        out_shape=[
            jax.ShapeDtypeStruct((tokens, features), bf),
            jax.ShapeDtypeStruct((2, tokens, features), jnp.float32),
            jax.ShapeDtypeStruct((3, 2, tokens, features), bf),
            jax.ShapeDtypeStruct((rel, features), bf),
            jax.ShapeDtypeStruct((tokens, features), bf),
        ],
        compiler_params=pltpu.CompilerParams(vmem_limit_bytes=56 << 20),
    )(owner, flags, q, *kvs, slots, cb, pb, ga)


def shifted(block, distance):
    count = lax.axis_size("ctx")
    return lax.ppermute(block, "ctx", [(i, (i + distance) % count) for i in range(count)])


def swapped(block, bit):
    return lax.ppermute(block, "head", [(i, i ^ bit) for i in range(lax.axis_size("head"))])


def body(
    query, key, value, pos_store, owner, block_mask, content_bias, pos_bias, out_weight, d_layer
):
    rows, features = query.shape
    window = block_mask.shape[1]
    slot_count = owner.shape[0]
    bf = jnp.bfloat16
    block_index = lax.axis_index("ctx")
    flags = block_mask[0] * (block_index >= jnp.arange(window)).astype(jnp.int32)

    own_pair = jnp.stack([key, value])
    lag1 = shifted(own_pair, 1)
    lag3 = shifted(own_pair, 3)
    slots = lax.all_to_all(
        jnp.broadcast_to(pos_store[None], (slot_count,) + pos_store.shape), "ctx", 0, 0
    ).reshape(-1, features)
    lag2 = shifted(lag1, 1)
    full_grad = lax.all_gather(d_layer, "head", axis=1, tiled=True)
    grad_attn = nt(full_grad, out_weight).astype(bf)

    grad_query, own, far, dist, attention = pair_call(
        owner, flags, query, [own_pair, lag1, lag2, lag3], slots,
        content_bias[None], pos_bias[None], grad_attn,
    )
    weight_term = tn(full_grad, attention).astype(bf)
    weight_parts = lax.all_to_all(weight_term.reshape(slot_count, -1, features), "ctx", 0, 0)
    pos_parts = lax.all_to_all(dist.reshape(slot_count, -1, features), "ctx", 0, 0)
    home3 = shifted(far[2], -3)
    step = (shifted(far[1], -1).astype(jnp.float32) + far[0].astype(jnp.float32)).astype(bf)
    home1 = shifted(step, -1)
    homed = own + home3.astype(jnp.float32) + home1.astype(jnp.float32)
    grad_pos = jnp.sum(pos_parts.astype(jnp.float32), axis=0).astype(bf)
    grad_weight = jnp.sum(weight_parts.astype(jnp.float32), axis=0).astype(bf).T
    return grad_query, homed[0].astype(bf), homed[1].astype(bf), grad_pos, grad_weight


def solution(mesh):
    spread = P("ctx", "head")
    return jax.shard_map(
        body,
        mesh=mesh,
        in_specs=(
            spread, spread, spread, spread, P(), P("ctx", None), P("head"), P("head"),
            P("head", None), spread,
        ),
        out_specs=(spread, spread, spread, spread, P("head", "ctx")),
        check_vma=False,
    )
```

```python
import functools

import jax
import jax.numpy as jnp
from jax import lax
from jax.experimental import pallas as pl
from jax.experimental.pallas import tpu as pltpu
from jax.sharding import PartitionSpec as P

HD = 64
LANES = 128
NEG = -1e30
ROW = 4
BF = jnp.bfloat16
F32 = jnp.float32


def nt(a, b):
    return lax.dot_general(a, b, (((1,), (1,)), ((), ())), preferred_element_type=F32)


def nn(a, b):
    return lax.dot_general(a, b, (((1,), (0,)), ((), ())), preferred_element_type=F32)


def tn(a, b):
    return lax.dot_general(a, b, (((0,), (0,)), ((), ())), preferred_element_type=F32)


def lanes():
    return lax.broadcasted_iota(jnp.int32, (1, LANES), 1)


def turned(block, shift=HD):
    return pltpu.roll(block.astype(F32), shift, 1)


def joined(low, high):
    return jnp.where(lanes() < HD, low.astype(F32), high.astype(F32))


def of_head(array, head):
    pair = array[:, head // 2 * LANES : (head // 2 + 1) * LANES]
    return turned(pair) if head % 2 else pair.astype(F32)


def halves(array, head):
    both = of_head(array, head)
    middle = both.shape[0] // 2
    return joined(both[:middle], turned(both[middle:]))


def whole_of(first, second):
    top = joined(first, turned(second))
    bottom = joined(turned(first), second)
    return jnp.concatenate([top, bottom], axis=0)


def anti_diagonal(size):
    row = lax.broadcasted_iota(jnp.int32, (size, size), 0)
    col = lax.broadcasted_iota(jnp.int32, (size, size), 1)
    return (row + col == size - 1).astype(F32).astype(BF)


def vmem_specs(count):
    return [pl.BlockSpec(memory_space=pltpu.VMEM)] * count


def smem_specs(count):
    return [pl.BlockSpec(memory_space=pltpu.SMEM)] * count


def any_specs(count):
    return [pl.BlockSpec(memory_space=pltpu.HBM)] * count


def whole_spec(shape):
    return pl.BlockSpec(shape, lambda *_: (0,) * len(shape))


def brought(pairs, sems):
    copies = [
        pltpu.make_async_copy(source, target, sems.at[i])
        for i, (source, target) in enumerate(pairs)
    ]
    for copy in copies:
        copy.start()
    for copy in copies:
        copy.wait()


def pack_kernel(mask_ref, q_in, k_in, v_in, pos_in, out_ref, q_ref, k_ref, v_ref, pos_ref, sems):
    brought([(q_in, q_ref), (k_in, k_ref), (v_in, v_ref), (pos_in, pos_ref)], sems)
    tokens = q_ref.shape[0]
    half = tokens // 2
    rows = pos_ref.shape[0] // 2
    flags = jnp.zeros((rows, LANES), F32)
    for lag in range(mask_ref.shape[1]):
        flags = jnp.where(lanes() == lag, mask_ref[0, lag].astype(F32), flags)
    for h in range(ROW):
        out_ref[h, :tokens, :] = joined(of_head(k_ref, h), turned(of_head(v_ref, h))).astype(BF)
        out_ref[h, tokens : tokens + half, :] = halves(q_ref, h).astype(BF)
        at = tokens + half
        out_ref[h, at : at + rows, :] = halves(pos_ref, h).astype(BF)
        out_ref[h, at + rows :, :] = flags.astype(BF)


def pack_call(mask, q, k, v, pos):
    tokens = q.shape[0]
    rows = tokens + tokens // 2 + pos.shape[0]
    return pl.pallas_call(
        pack_kernel,
        in_specs=smem_specs(1) + any_specs(4),
        out_shape=pltpu.HBM((ROW, rows, LANES), BF),
        scratch_shapes=[pltpu.VMEM(a.shape, BF) for a in (q, k, v, pos)]
        + [pltpu.SemaphoreType.DMA((4,))],
        compiler_params=pltpu.CompilerParams(vmem_limit_bytes=60 << 20),
    )(mask, q, k, v, pos)


def mix_kernel(
    place_ref, g0_in, g1_in, g2_in, g3_in, weight_in, out_ref, g0, g1, g2, g3, weight_ref, sems
):
    brought(
        [(g0_in, g0), (g1_in, g1), (g2_in, g2), (g3_in, g3), (weight_in, weight_ref)], sems
    )
    features = g0.shape[1]
    mixed = None
    for b, grad in enumerate((g0, g1, g2, g3)):
        at = pl.multiple_of((place_ref[0] ^ b) * features, features)
        part = nt(grad[...], weight_ref[:, pl.ds(at, features)])
        mixed = part if mixed is None else mixed + part
    mixed = mixed.astype(BF)
    for h in range(ROW):
        out_ref[h] = halves(mixed, h).astype(BF)


def mix_call(place, grads, out_weight):
    tokens = grads[0].shape[0]
    return pl.pallas_call(
        mix_kernel,
        in_specs=smem_specs(1) + any_specs(5),
        out_shape=pltpu.HBM((ROW, tokens // 2, LANES), BF),
        scratch_shapes=[pltpu.VMEM(a.shape, BF) for a in (*grads, out_weight)]
        + [pltpu.SemaphoreType.DMA((5,))],
        compiler_params=pltpu.CompilerParams(vmem_limit_bytes=60 << 20),
    )(place, *grads, out_weight)


def key_pairs(row_in, halo_in, keys, query, tokens):
    pairs = [(halo_in.at[b], keys.at[b * tokens : (b + 1) * tokens]) for b in range(ROW - 1)]
    for b in range(ROW):
        at = (ROW - 1 + b) * tokens
        pairs.append((row_in.at[b, 0:tokens], keys.at[at : at + tokens]))
        pairs.append((row_in.at[b, tokens : tokens + tokens // 2], query.at[b]))
    return pairs


def core_kernel(
    owner_ref, flag_ref, row_in, halo_in, slots_in, ga_in, cb_ref, pb_ref,
    near_ref, own_ref, far_ref, dpos_ref,
    keys, queries, slots_ref, ga_ref, table, flipped, grads, dist, sems,
):
    tokens = halo_in.shape[1]
    half = tokens // 2
    span = ROW * tokens
    wide = span + half
    block = pl.program_id(0)
    anti = anti_diagonal(half)

    @pl.when(block == 0)
    def _():
        pairs = key_pairs(row_in, halo_in, keys, queries, tokens)
        brought(pairs + [(slots_in, slots_ref), (ga_in, ga_ref)], sems)
        grads[...] = jnp.zeros_like(grads)
        dist[...] = jnp.zeros_like(dist)
        table[0:tokens, :] = jnp.zeros((tokens, LANES), BF)
        count, rows = slots_ref.shape[:2]
        for d in range(count):
            both = slots_ref[owner_ref[d]]
            at = tokens + 2 * d * rows
            table[at : at + rows, :] = both
            table[at + rows : at + 2 * rows, :] = turned(both).astype(BF)
        parts = (tokens + span) // half
        for i in range(parts):
            flipped[(parts - 1 - i) * half : (parts - i) * half, :] = nn(
                anti, table[i * half : (i + 1) * half, :]
            ).astype(BF)

    lane = lanes()
    low = lane < HD
    scale = jnp.asarray(0.125, BF)
    starts = [pl.multiple_of((block + w) * tokens, tokens) for w in range(ROW)]
    kept = []
    dqs = []
    for r in range(2):
        query = queries[block].astype(F32)
        ga = ga_ref[block].astype(F32)
        query = turned(query) if r == 1 else query
        ga = turned(ga) if r == 0 else ga
        ga = jnp.where(low, 0.0, ga)
        cq = jnp.where(low, query + cb_ref[...], 0.0).astype(BF)
        pq = jnp.where(low, query + pb_ref[...], 0.0).astype(BF)
        cqs = cq * scale
        pqs = pq * scale
        base = half * (1 - r)
        rel = nt(pqs, flipped[base : base + wide, :])
        rel = pltpu.roll(rel, span + 1, 1, stride=1, stride_axis=0)
        scores = []
        for w in range(ROW):
            s = nt(cqs, keys[pl.ds(starts[w], tokens), :]) + rel[:, w * tokens : (w + 1) * tokens]
            if w == ROW - 1:
                row = lax.broadcasted_iota(jnp.int32, (half, tokens), 0) + r * half
                col = lax.broadcasted_iota(jnp.int32, (half, tokens), 1)
                s = jnp.where(col <= row, s, NEG)
            else:
                s = jnp.where(flag_ref[block, ROW - 1 - w] == 1, s, NEG)
            scores.append(s)
        top = functools.reduce(jnp.maximum, [jnp.max(s, axis=1, keepdims=True) for s in scores])
        weights = [jnp.exp(s - top) for s in scores]
        total = functools.reduce(jnp.add, [jnp.sum(e, axis=1, keepdims=True) for e in weights])
        inv = 1.0 / total
        probs = [e * inv for e in weights]
        lows = [p.astype(BF) for p in probs]
        att = None
        for w in range(ROW):
            part = nn(lows[w], keys[pl.ds(starts[w], tokens), :])
            att = part if att is None else att + part
        att = att.astype(BF).astype(F32)
        kept.append(turned(att) if r == 0 else att)
        dot = jnp.sum(ga * att, axis=1, keepdims=True)
        ga = ga.astype(BF)
        flips = [None] * (2 * ROW)
        acc = None
        for w in range(ROW):
            window = keys[pl.ds(starts[w], tokens), :]
            ds = (0.125 * probs[w] * (nt(ga, window) - dot)).astype(BF)
            grads[:, pl.ds(starts[w], tokens)] += tn(cq, ds) + tn(ga, lows[w])
            part = nn(ds, window)
            acc = part if acc is None else acc + part
            for x in range(2):
                flips[2 * ROW - 1 - (2 * w + x)] = nn(ds[:, x * half : (x + 1) * half], anti)
        spread = jnp.concatenate(flips + [jnp.zeros((half, half), F32)], axis=1)
        spread = pltpu.roll(spread, 1, 1, stride=1, stride_axis=0).astype(BF)
        start = half * r
        acc = acc + nn(spread, table[start : start + wide, :])
        dist[:, start : start + wide] += tn(pq, spread)
        dqs.append(turned(acc) if r == 1 else acc)
    near_ref[block, :half, :] = joined(kept[0], kept[1]).astype(BF)
    near_ref[block, half:, :] = joined(dqs[0], dqs[1]).astype(BF)

    @pl.when(block == ROW - 1)
    def _():
        for b in range(ROW - 1):
            far_ref[b] = grads[:, b * tokens : (b + 1) * tokens].T.astype(BF)
        for b in range(ROW):
            at = (ROW - 1 + b) * tokens
            own_ref[b] = grads[:, at : at + tokens].T
        count, rows = dpos_ref.shape[:2]
        table_grad = dist[:, tokens:].T
        other = pltpu.roll(table_grad, HD, 1)
        for d in range(count):
            at = 2 * d * rows
            dpos_ref[owner_ref[d]] = joined(
                table_grad[at : at + rows], other[at + rows : at + 2 * rows]
            ).astype(BF)


def core_call(owner, flags, row, halo, slots, ga, cb, pb):
    tokens = halo.shape[1]
    half = tokens // 2
    slot_count, packed_rows = slots.shape[:2]
    rel = slot_count * packed_rows * 2
    shapes = [
        ((ROW, tokens, LANES), BF), ((ROW, tokens, LANES), F32), ((ROW - 1, tokens, LANES), BF),
        ((slot_count, packed_rows, LANES), BF),
    ]
    return pl.pallas_call(
        core_kernel,
        grid=(ROW,),
        in_specs=smem_specs(2) + any_specs(4) + vmem_specs(2),
        out_specs=[whole_spec(shape) for shape, _ in shapes],
        out_shape=[pltpu.HBM(shape, dtype) for shape, dtype in shapes],
        scratch_shapes=[
            pltpu.VMEM(((2 * ROW - 1) * tokens, LANES), BF),
            pltpu.VMEM((ROW, half, LANES), BF),
            pltpu.VMEM(slots.shape, BF),
            pltpu.VMEM((ROW, half, LANES), BF),
            pltpu.VMEM((tokens + rel, LANES), BF),
            pltpu.VMEM((tokens + rel, LANES), BF),
            pltpu.VMEM((LANES, (2 * ROW - 1) * tokens), F32),
            pltpu.VMEM((LANES, tokens + rel), F32),
            pltpu.SemaphoreType.DMA((3 * ROW + 1,)),
        ],
        compiler_params=pltpu.CompilerParams(vmem_limit_bytes=60 << 20),
        cost_estimate=pl.CostEstimate(
            flops=40_000_000_000, bytes_accessed=8_000_000, transcendentals=0
        ),
    )(owner, flags, row, halo, slots, ga, cb, pb)


def weight_kernel(
    place_ref, att_in, g0_in, g1_in, g2_in, g3_in, dpos_in, out_ref,
    att_ref, g0, g1, g2, g3, dpos_ref, sems,
):
    half = att_ref.shape[1]
    sources = [att_in.at[:, 0:half], g0_in, g1_in, g2_in, g3_in, dpos_in]
    brought(zip(sources, [att_ref, g0, g1, g2, g3, dpos_ref]), sems)
    rows = dpos_ref.shape[1]
    features = g0.shape[1]
    chunks = features // rows
    out_ref[:, :rows, :] = dpos_ref[...]
    for pair in range(features // LANES):
        att = whole_of(att_ref[2 * pair], att_ref[2 * pair + 1]).astype(BF)
        at = rows * (1 + pair)
        for b, grad in enumerate((g0, g1, g2, g3)):
            term = tn(att, grad[...]).T.astype(BF)
            out_ref[pl.ds((place_ref[0] ^ b) * chunks, chunks), at : at + rows, :] = term.reshape(
                chunks, rows, LANES
            )


def weight_call(place, att, grads, dpos):
    slot_count, rows = dpos.shape[:2]
    pairs = grads[0].shape[1] // LANES
    return pl.pallas_call(
        weight_kernel,
        in_specs=smem_specs(1) + any_specs(6),
        scratch_shapes=[pltpu.VMEM((ROW, grads[0].shape[0] // 2, LANES), BF)]
        + [pltpu.VMEM(a.shape, BF) for a in (*grads, dpos)]
        + [pltpu.SemaphoreType.DMA((6,))],
        out_shape=pltpu.HBM((slot_count, rows * (1 + pairs), LANES), BF),
        compiler_params=pltpu.CompilerParams(vmem_limit_bytes=60 << 20),
    )(place, att, *grads, dpos)


def meet_kernel(own_in, far_in, parts_in, out_ref, own_ref, far_ref, parts_ref, sems):
    sources = [own_in, far_in, parts_in]
    brought(zip(sources, [own_ref, far_ref, parts_ref]), sems)
    tokens = own_ref.shape[1]
    for b in range(ROW):
        grad = own_ref[b]
        if b > 0:
            grad = grad + far_ref[b - 1].astype(F32)
        out_ref[b, :tokens, :] = grad.astype(BF)
        total = parts_ref[0, b].astype(F32)
        for z in range(1, parts_ref.shape[0]):
            total = total + parts_ref[z, b].astype(F32)
        out_ref[b, tokens:, :] = total.astype(BF)


def meet_call(own, far, parts):
    rows = own.shape[1] + parts.shape[2]
    return pl.pallas_call(
        meet_kernel,
        in_specs=any_specs(3),
        out_shape=pltpu.HBM((ROW, rows, LANES), BF),
        scratch_shapes=[pltpu.VMEM(a.shape, a.dtype) for a in (own, far, parts)]
        + [pltpu.SemaphoreType.DMA((3,))],
        compiler_params=pltpu.CompilerParams(vmem_limit_bytes=60 << 20),
    )(own, far, parts)


def final_kernel(
    in_in, near_in, dq_ref, dk_ref, dv_ref, dpos_ref, dw_ref, in_ref, near_ref, sems
):
    tokens = dq_ref.shape[0]
    brought([(in_in, in_ref), (near_in.at[:, tokens // 2 :], near_ref)], sems)
    rows = dpos_ref.shape[0] // 2
    at = tokens
    for pair in range(ROW // 2):
        cols = slice(pair * LANES, (pair + 1) * LANES)
        dq_ref[:, cols] = whole_of(near_ref[2 * pair], near_ref[2 * pair + 1]).astype(BF)
        first, second = in_ref.at[2 * pair], in_ref.at[2 * pair + 1]
        a, b = first[:at, :], second[:at, :]
        dk_ref[:, cols] = joined(a, turned(b)).astype(BF)
        dv_ref[:, cols] = joined(turned(a), b).astype(BF)
        dpos_ref[:, cols] = whole_of(first[at : at + rows, :], second[at : at + rows, :]).astype(BF)
        lo = at + rows * (1 + pair)
        total = in_ref[0, lo : lo + rows, :].astype(F32)
        for x in range(1, ROW):
            total = total + in_ref[x, lo : lo + rows, :].astype(F32)
        dw_ref[:, cols] = total.astype(BF)


def final_call(arrived, near, features, slot_rows, out_rows):
    tokens = near.shape[1]
    shapes = [(tokens, features)] * 3 + [(slot_rows, features), (out_rows, features)]
    return pl.pallas_call(
        final_kernel,
        in_specs=any_specs(2),
        out_shape=[jax.ShapeDtypeStruct(shape, BF) for shape in shapes],
        scratch_shapes=[
            pltpu.VMEM(arrived.shape, BF),
            pltpu.VMEM((ROW, tokens // 2, LANES), BF),
            pltpu.SemaphoreType.DMA((2,)),
        ],
        compiler_params=pltpu.CompilerParams(vmem_limit_bytes=60 << 20),
    )(arrived, near)


def shifted(block, distance):
    count = lax.axis_size("ctx")
    return lax.ppermute(block, "ctx", [(i, (i + distance) % count) for i in range(count)])


def swapped(block, bit):
    return lax.ppermute(block, "head", [(i, i ^ bit) for i in range(lax.axis_size("head"))])


def in_row(block):
    count = lax.axis_size("ctx")
    groups = [list(range(r, r + ROW)) for r in range(0, count, ROW)]
    return lax.all_to_all(block, "ctx", 0, 0, axis_index_groups=groups)


def in_column(block):
    count = lax.axis_size("ctx")
    groups = [list(range(x, count, ROW)) for x in range(ROW)]
    return lax.all_to_all(block, "ctx", 0, 0, axis_index_groups=groups)


def body(
    query, key, value, pos_store, owner, block_mask, content_bias, pos_bias, out_weight, d_layer
):
    tokens, features = query.shape
    window = block_mask.shape[1]
    slot_count = owner.shape[0]
    slot_rows = pos_store.shape[0]
    half = tokens // 2
    block_index = lax.axis_index("ctx")
    place = lax.axis_index("head").astype(jnp.int32)[None]
    mine = block_index % ROW

    def bias_of(bias):
        part = lax.dynamic_slice_in_dim(bias, mine * HD, HD)
        return jnp.pad(part, (0, LANES - HD))[None]

    cb, pb = bias_of(content_bias), bias_of(pos_bias)
    across = swapped(d_layer, 2)
    row = in_row(pack_call(block_mask, query, key, value, pos_store))
    halo = shifted(row[1:, :tokens], ROW)
    at = tokens + half
    pos = row[:, at : at + slot_rows // 2]
    grads = [d_layer, swapped(d_layer, 1), across, swapped(across, 1)]
    mixed = mix_call(place, grads, out_weight)
    ga = in_row(mixed)
    pos, halo, ga = lax.optimization_barrier((pos, halo, ga))
    slots = in_column(jnp.broadcast_to(pos[None], (slot_count // ROW,) + pos.shape))
    slots = slots.reshape(slot_count, slot_rows // 2, LANES)
    flags = row[:, at + slot_rows // 2, :window].astype(jnp.int32)
    blocks = block_index - mine + jnp.arange(ROW)
    flags = flags * (blocks[:, None] >= jnp.arange(window)[None]).astype(jnp.int32)

    near, own, far, dpos = core_call(owner, flags, row, halo, slots, ga, cb, pb)
    back = shifted(far, -ROW)
    near = in_row(near)
    near, back = lax.optimization_barrier((near, back))
    sums = weight_call(place, near, grads, dpos)
    parts = in_column(sums.reshape((slot_count // ROW, ROW) + sums.shape[1:]))
    arrived = in_row(meet_call(own, back, parts))
    grad_query, grad_key, grad_value, grad_pos, grad_weight = final_call(
        arrived, near, features, slot_rows, slot_rows // 2
    )
    return grad_query, grad_key, grad_value, grad_pos, grad_weight.T


def solution(mesh):
    spread = P("ctx", "head")
    return jax.shard_map(
        body,
        mesh=mesh,
        in_specs=(
            spread, spread, spread, spread, P(), P("ctx", None), P("head"), P("head"),
            P("head", None), spread,
        ),
        out_specs=(spread, spread, spread, spread, P("head", "ctx")),
        check_vma=False,
    )
```

```python
import functools

import jax
import jax.numpy as jnp
from jax import lax
from jax.experimental import pallas as pl
from jax.experimental.pallas import tpu as pltpu
from jax.sharding import PartitionSpec as P

HD = 64
LANES = 128
NEG = -1e30
ROW = 4
BF = jnp.bfloat16
F32 = jnp.float32


def nt(a, b):
    return lax.dot_general(a, b, (((1,), (1,)), ((), ())), preferred_element_type=F32)


def nn(a, b):
    return lax.dot_general(a, b, (((1,), (0,)), ((), ())), preferred_element_type=F32)


def tn(a, b):
    return lax.dot_general(a, b, (((0,), (0,)), ((), ())), preferred_element_type=F32)


def lanes():
    return lax.broadcasted_iota(jnp.int32, (1, LANES), 1)


def turned(block, shift=HD):
    return pltpu.roll(block.astype(F32), shift, 1)


def joined(low, high):
    return jnp.where(lanes() < HD, low.astype(F32), high.astype(F32))


def of_head(array, head):
    pair = array[:, head // 2 * LANES : (head // 2 + 1) * LANES]
    return turned(pair) if head % 2 else pair.astype(F32)


def halves(array, head):
    both = of_head(array, head)
    middle = both.shape[0] // 2
    return joined(both[:middle], turned(both[middle:]))


def whole_of(first, second):
    top = joined(first, turned(second))
    bottom = joined(turned(first), second)
    return jnp.concatenate([top, bottom], axis=0)


def anti_diagonal(size):
    row = lax.broadcasted_iota(jnp.int32, (size, size), 0)
    col = lax.broadcasted_iota(jnp.int32, (size, size), 1)
    return (row + col == size - 1).astype(F32).astype(BF)


def vmem_specs(count):
    return [pl.BlockSpec(memory_space=pltpu.VMEM)] * count


def smem_specs(count):
    return [pl.BlockSpec(memory_space=pltpu.SMEM)] * count


def any_specs(count):
    return [pl.BlockSpec(memory_space=pl.ANY)] * count


def hbm_specs(count):
    return [pl.BlockSpec(memory_space=pltpu.HBM)] * count


def whole_spec(shape):
    return pl.BlockSpec(shape, lambda *_: (0,) * len(shape))


def brought(pairs, sems):
    copies = [
        pltpu.make_async_copy(source, target, sems.at[i])
        for i, (source, target) in enumerate(pairs)
    ]
    for copy in copies:
        copy.start()
    for copy in copies:
        copy.wait()


def pack_kernel(mask_ref, q_in, k_in, v_in, pos_in, out_ref, q_ref, k_ref, v_ref, pos_ref, sems):
    brought([(q_in, q_ref), (k_in, k_ref), (v_in, v_ref), (pos_in, pos_ref)], sems)
    tokens = q_ref.shape[0]
    half = tokens // 2
    rows = pos_ref.shape[0] // 2
    flags = jnp.zeros((rows, LANES), F32)
    for lag in range(mask_ref.shape[1]):
        flags = jnp.where(lanes() == lag, mask_ref[0, lag].astype(F32), flags)
    for h in range(ROW):
        out_ref[h, :tokens, :] = joined(of_head(k_ref, h), turned(of_head(v_ref, h))).astype(BF)
        out_ref[h, tokens : tokens + half, :] = halves(q_ref, h).astype(BF)
        at = tokens + half
        out_ref[h, at : at + rows, :] = halves(pos_ref, h).astype(BF)
        out_ref[h, at + rows :, :] = flags.astype(BF)


def pack_call(mask, q, k, v, pos):
    tokens = q.shape[0]
    rows = tokens + tokens // 2 + pos.shape[0]
    return pl.pallas_call(
        pack_kernel,
        in_specs=smem_specs(1) + hbm_specs(4),
        out_shape=pltpu.HBM((ROW, rows, LANES), BF),
        scratch_shapes=[pltpu.VMEM(a.shape, BF) for a in (q, k, v, pos)]
        + [pltpu.SemaphoreType.DMA((4,))],
        compiler_params=pltpu.CompilerParams(vmem_limit_bytes=60 << 20),
    )(mask, q, k, v, pos)


def mix_kernel(
    g0_in, g1_in, g2_in, g3_in, weight_in, out_ref, g0, g1, g2, g3, weight_ref, sems
):
    brought(
        [(g0_in, g0), (g1_in, g1), (g2_in, g2), (g3_in, g3), (weight_in, weight_ref)], sems
    )
    features = g0.shape[1]
    mixed = None
    for b, grad in enumerate((g0, g1, g2, g3)):
        at = pl.multiple_of((lax.axis_index("head") ^ b) * features, features)
        part = nt(grad[...], weight_ref[:, pl.ds(at, features)])
        mixed = part if mixed is None else mixed + part
    mixed = mixed.astype(BF)
    for h in range(ROW):
        out_ref[h] = halves(mixed, h).astype(BF)


def mix_call(grads, out_weight):
    tokens = grads[0].shape[0]
    return pl.pallas_call(
        mix_kernel,
        in_specs=any_specs(5),
        out_shape=pltpu.HBM((ROW, tokens // 2, LANES), BF),
        scratch_shapes=[pltpu.VMEM(a.shape, BF) for a in (*grads, out_weight)]
        + [pltpu.SemaphoreType.DMA((5,))],
        compiler_params=pltpu.CompilerParams(vmem_limit_bytes=16 << 20),
    )(*grads, out_weight)


def key_pairs(row_in, halo_in, keys, query, tokens):
    pairs = [(halo_in.at[b], keys.at[b * tokens : (b + 1) * tokens]) for b in range(ROW - 1)]
    for b in range(ROW):
        at = (ROW - 1 + b) * tokens
        pairs.append((row_in.at[b, 0:tokens], keys.at[at : at + tokens]))
        pairs.append((row_in.at[b, tokens : tokens + tokens // 2], query.at[b]))
    return pairs


def core_kernel(
    owner_ref, row_in, halo_in, s0_in, s1_in, s2_in, s3_in, ga_in, cb_in, pb_in,
    near_ref, own_ref, far_ref, dpos_ref,
    keys, queries, slots_ref, ga_ref, table, flipped, grads, dist,
    score_ref, rel_ref, low_ref, ds_ref, spread_ref, dot_ref, flag_ref, cb_ref, pb_ref, sems,
):
    tokens = halo_in.shape[1]
    half = tokens // 2
    span = ROW * tokens
    wide = span + half
    block = pl.program_id(0)
    anti = anti_diagonal(half)

    @pl.when(block == 0)
    def _():
        pairs = key_pairs(row_in, halo_in, keys, queries, tokens)
        pairs += [(part, slots_ref.at[i]) for i, part in enumerate((s0_in, s1_in, s2_in, s3_in))]
        at = tokens + half + slots_ref.shape[3]
        pairs += [(ga_in, ga_ref), (row_in.at[:, at : at + 16], flag_ref)]
        brought(pairs, sems)
        turn = (ROW - (lax.axis_index("ctx") & 3)) * HD % cb_in.shape[1]
        for bias_in, bias_ref in ((cb_in, cb_ref), (pb_in, pb_ref)):
            bias = jnp.broadcast_to(bias_in[...], (8, bias_in.shape[1]))
            bias_ref[...] = pltpu.roll(bias, turn, 1)[0:1, :LANES]
        grads[...] = jnp.zeros_like(grads)
        dist[...] = jnp.zeros_like(dist)
        table[0:tokens, :] = jnp.zeros((tokens, LANES), BF)
        count, rows = owner_ref.shape[0], slots_ref.shape[3]
        for d in range(count):
            slot = owner_ref[d]
            apart = (slot >> 2) ^ (lax.axis_index("ctx") >> 2)
            both = slots_ref[apart & 3, apart >> 2, slot & 3]
            at = tokens + 2 * d * rows
            table[at : at + rows, :] = both
            table[at + rows : at + 2 * rows, :] = turned(both).astype(BF)
        parts = (tokens + span) // half
        for i in range(parts):
            flipped[(parts - 1 - i) * half : (parts - i) * half, :] = nn(
                anti, table[i * half : (i + 1) * half, :]
            ).astype(BF)

    lane = lanes()
    low = lane < HD
    scale = jnp.asarray(0.125, BF)
    starts = [pl.multiple_of((block + w) * tokens, tokens) for w in range(ROW)]
    kept = []
    dqs = []
    chunk = 16
    groups = [slice(c, c + chunk) for c in range(0, half, chunk)]
    barred = []
    for lag in range(ROW - 1, 0, -1):
        there = (lax.axis_index("ctx") & ~3) + block >= lag
        flag = flag_ref[block, 0:1, lag : lag + 1].astype(F32)
        barred.append(jnp.where(there & (flag > 0.5), 0.0, NEG))
    state = [{}, {}]

    def first(r):
        query = queries[block].astype(F32)
        ga = ga_ref[block].astype(F32)
        query = turned(query) if r == 1 else query
        ga = turned(ga) if r == 0 else ga
        ga = jnp.where(low, 0.0, ga)
        cq = jnp.where(low, query + cb_ref[...], 0.0).astype(BF)
        pq = jnp.where(low, query + pb_ref[...], 0.0).astype(BF)
        state[r].update(ga=ga, gal=ga.astype(BF), cq=cq, pq=pq)
        base = half * (1 - r)
        rel_ref[r] = nt(pq * scale, flipped[base : base + wide, :])
        cqs = cq * scale
        for w in range(ROW):
            score_ref[r, :, w * tokens : (w + 1) * tokens] = nt(
                cqs, keys[pl.ds(starts[w], tokens), :]
            )

    def soften(r):
        for g in groups:
            moved = pltpu.roll(
                rel_ref[r, g, :], (span + 1 + g.start) % wide, 1, stride=1, stride_axis=0
            )
            scores = []
            for w in range(ROW):
                cols = slice(w * tokens, (w + 1) * tokens)
                s = score_ref[r, g, cols] + moved[:, cols]
                if w == ROW - 1:
                    row = lax.broadcasted_iota(jnp.int32, (chunk, tokens), 0) + r * half + g.start
                    col = lax.broadcasted_iota(jnp.int32, (chunk, tokens), 1)
                    s = jnp.where(col <= row, s, NEG)
                else:
                    s = s + barred[w]
                scores.append(s)
            top = functools.reduce(jnp.maximum, scores)
            top = jnp.max(top, axis=1, keepdims=True)
            weights = [jnp.exp(s - top) for s in scores]
            total = functools.reduce(jnp.add, weights)
            inv = 1.0 / jnp.sum(total, axis=1, keepdims=True)
            for w in range(ROW):
                cols = slice(w * tokens, (w + 1) * tokens)
                p = weights[w] * inv
                score_ref[r, g, cols] = p
                low_ref[r, g, cols] = p.astype(BF)

    def second(r):
        att = None
        for w in range(ROW):
            cols = slice(w * tokens, (w + 1) * tokens)
            part = nn(low_ref[r, :, cols], keys[pl.ds(starts[w], tokens), :])
            att = part if att is None else att + part
        att = att.astype(BF).astype(F32)
        state[r]["att"] = turned(att) if r == 0 else att
        dot = jnp.sum(state[r]["ga"] * att, axis=1, keepdims=True)
        dot_ref[r] = jnp.broadcast_to(dot, (half, LANES))
        for w in range(ROW):
            cols = slice(w * tokens, (w + 1) * tokens)
            rel_ref[r, :, cols] = nt(state[r]["gal"], keys[pl.ds(starts[w], tokens), :])

    def steepen(r):
        for g in groups:
            dot = dot_ref[r, g, 0:1]
            for w in range(ROW):
                cols = slice(w * tokens, (w + 1) * tokens)
                ds = 0.125 * score_ref[r, g, cols] * (rel_ref[r, g, cols] - dot)
                ds_ref[r, g, cols] = ds.astype(BF)

    def third(r):
        acc = None
        for w in range(ROW):
            cols = slice(w * tokens, (w + 1) * tokens)
            ds = ds_ref[r, :, cols]
            for x in range(2):
                at = (2 * ROW - 1 - (2 * w + x)) * half
                rel_ref[r, :, at : at + half] = nn(ds[:, x * half : (x + 1) * half], anti)
        rel_ref[r, :, span:] = jnp.zeros((half, wide - span), F32)
        for w in range(ROW):
            cols = slice(w * tokens, (w + 1) * tokens)
            ds = ds_ref[r, :, cols]
            grads[:, pl.ds(starts[w], tokens)] += tn(state[r]["cq"], ds) + tn(
                state[r]["gal"], low_ref[r, :, cols]
            )
            part = nn(ds, keys[pl.ds(starts[w], tokens), :])
            acc = part if acc is None else acc + part
        state[r]["acc"] = acc

    def slant(r):
        for g in groups:
            spread_ref[r, g, :] = pltpu.roll(
                rel_ref[r, g, :], 1 + g.start, 1, stride=1, stride_axis=0
            ).astype(BF)

    def fourth(r):
        start = half * r
        acc = state[r]["acc"] + nn(spread_ref[r], table[start : start + wide, :])
        dist[:, start : start + wide] += tn(state[r]["pq"], spread_ref[r])
        state[r]["acc"] = turned(acc) if r == 1 else acc

    first(0)
    for stage, other in (
        (soften, first), (second, soften), (steepen, second), (third, steepen), (slant, third),
        (fourth, slant),
    ):
        stage(0)
        other(1)
    fourth(1)
    kept = [part["att"] for part in state]
    dqs = [part["acc"] for part in state]
    near_ref[block, :half, :] = joined(kept[0], kept[1]).astype(BF)
    near_ref[block, half:, :] = joined(dqs[0], dqs[1]).astype(BF)

    @pl.when(block == ROW - 1)
    def _():
        for b in range(ROW - 1):
            far_ref[b] = grads[:, b * tokens : (b + 1) * tokens].T.astype(BF)
        for b in range(ROW):
            at = (ROW - 1 + b) * tokens
            own_ref[b] = grads[:, at : at + tokens].T
        count, rows = dpos_ref.shape[:2]
        table_grad = dist[:, tokens:].T
        other = pltpu.roll(table_grad, HD, 1)
        for d in range(count):
            at = 2 * d * rows
            dpos_ref[owner_ref[d]] = joined(
                table_grad[at : at + rows], other[at + rows : at + 2 * rows]
            ).astype(BF)


def core_call(owner, row, halo, slots, ga, cb, pb):
    tokens = halo.shape[1]
    half = tokens // 2
    slot_count = owner.shape[0]
    packed_rows = slots[0].shape[2]
    rel = slot_count * packed_rows * 2
    shapes = [
        ((ROW, tokens, LANES), BF), ((ROW, tokens, LANES), F32), ((ROW - 1, tokens, LANES), BF),
        ((slot_count, packed_rows, LANES), BF),
    ]
    return pl.pallas_call(
        core_kernel,
        grid=(ROW,),
        in_specs=smem_specs(1) + any_specs(7) + vmem_specs(2),
        out_specs=[whole_spec(shape) for shape, _ in shapes],
        out_shape=[pltpu.HBM(shape, dtype) for shape, dtype in shapes],
        scratch_shapes=[
            pltpu.VMEM(((2 * ROW - 1) * tokens, LANES), BF),
            pltpu.VMEM((ROW, half, LANES), BF),
            pltpu.VMEM((4,) + slots[0].shape, BF),
            pltpu.VMEM((ROW, half, LANES), BF),
            pltpu.VMEM((tokens + rel, LANES), BF),
            pltpu.VMEM((tokens + rel, LANES), BF),
            pltpu.VMEM((LANES, (2 * ROW - 1) * tokens), F32),
            pltpu.VMEM((LANES, tokens + rel), F32),
            pltpu.VMEM((2, half, ROW * tokens), F32),
            pltpu.VMEM((2, half, ROW * tokens + half), F32),
            pltpu.VMEM((2, half, ROW * tokens), BF),
            pltpu.VMEM((2, half, ROW * tokens), BF),
            pltpu.VMEM((2, half, ROW * tokens + half), BF),
            pltpu.VMEM((2, half, LANES), F32),
            pltpu.VMEM((ROW, 16, LANES), BF),
            pltpu.VMEM((1, LANES), F32),
            pltpu.VMEM((1, LANES), F32),
            pltpu.SemaphoreType.DMA((3 * ROW + 5,)),
        ],
        compiler_params=pltpu.CompilerParams(vmem_limit_bytes=60 << 20),
        cost_estimate=pl.CostEstimate(
            flops=40_000_000_000, bytes_accessed=8_000_000, transcendentals=0
        ),
    )(owner, row, halo, *slots, ga, cb, pb)


def weight_kernel(
    att_in, g0_in, g1_in, g2_in, g3_in, dpos_in, out_ref,
    att_ref, g0, g1, g2, g3, dpos_ref, sems,
):
    half = att_ref.shape[1]
    sources = [att_in.at[:, 0:half], g0_in, g1_in, g2_in, g3_in, dpos_in]
    brought(zip(sources, [att_ref, g0, g1, g2, g3, dpos_ref]), sems)
    rows = dpos_ref.shape[1]
    features = g0.shape[1]
    chunks = features // rows
    out_ref[:, :rows, :] = dpos_ref[...]
    for pair in range(features // LANES):
        att = whole_of(att_ref[2 * pair], att_ref[2 * pair + 1]).astype(BF)
        at = rows * (1 + pair)
        for b, grad in enumerate((g0, g1, g2, g3)):
            term = tn(att, grad[...]).T.astype(BF)
            out_ref[pl.ds((lax.axis_index("head") ^ b) * chunks, chunks), at : at + rows, :] = term.reshape(
                chunks, rows, LANES
            )


def weight_call(att, grads, dpos):
    slot_count, rows = dpos.shape[:2]
    pairs = grads[0].shape[1] // LANES
    return pl.pallas_call(
        weight_kernel,
        in_specs=any_specs(6),
        scratch_shapes=[pltpu.VMEM((ROW, grads[0].shape[0] // 2, LANES), BF)]
        + [pltpu.VMEM(a.shape, BF) for a in (*grads, dpos)]
        + [pltpu.SemaphoreType.DMA((6,))],
        out_shape=pltpu.HBM((slot_count, rows * (1 + pairs), LANES), BF),
        compiler_params=pltpu.CompilerParams(vmem_limit_bytes=16 << 20),
    )(att, *grads, dpos)


def meet_kernel(own_in, far_in, parts_in, out_ref, own_ref, far_ref, parts_ref, sems):
    sources = [own_in, far_in, parts_in]
    brought(zip(sources, [own_ref, far_ref, parts_ref]), sems)
    tokens = own_ref.shape[1]
    for b in range(ROW):
        grad = own_ref[b]
        if b > 0:
            grad = grad + far_ref[b - 1].astype(F32)
        out_ref[b, :tokens, :] = grad.astype(BF)
        total = parts_ref[0, b].astype(F32)
        for z in range(1, parts_ref.shape[0]):
            total = total + parts_ref[z, b].astype(F32)
        out_ref[b, tokens:, :] = total.astype(BF)


def meet_call(own, far, parts):
    rows = own.shape[1] + parts.shape[2]
    return pl.pallas_call(
        meet_kernel,
        in_specs=any_specs(3),
        out_shape=pltpu.HBM((ROW, rows, LANES), BF),
        scratch_shapes=[pltpu.VMEM(a.shape, a.dtype) for a in (own, far, parts)]
        + [pltpu.SemaphoreType.DMA((3,))],
        compiler_params=pltpu.CompilerParams(vmem_limit_bytes=16 << 20),
    )(own, far, parts)


def final_kernel(
    in_in, near_in, dq_ref, dk_ref, dv_ref, dpos_ref, dw_ref, in_ref, near_ref, sems
):
    tokens = dq_ref.shape[0]
    brought([(in_in, in_ref), (near_in.at[:, tokens // 2 :], near_ref)], sems)
    rows = dpos_ref.shape[0] // 2
    at = tokens
    for pair in range(ROW // 2):
        cols = slice(pair * LANES, (pair + 1) * LANES)
        dq_ref[:, cols] = whole_of(near_ref[2 * pair], near_ref[2 * pair + 1]).astype(BF)
        first, second = in_ref.at[2 * pair], in_ref.at[2 * pair + 1]
        a, b = first[:at, :], second[:at, :]
        dk_ref[:, cols] = joined(a, turned(b)).astype(BF)
        dv_ref[:, cols] = joined(turned(a), b).astype(BF)
        dpos_ref[:, cols] = whole_of(first[at : at + rows, :], second[at : at + rows, :]).astype(BF)
        lo = at + rows * (1 + pair)
        total = in_ref[0, lo : lo + rows, :].astype(F32)
        for x in range(1, ROW):
            total = total + in_ref[x, lo : lo + rows, :].astype(F32)
        dw_ref[:, cols] = total.astype(BF)


def final_call(arrived, near, features, slot_rows, out_rows):
    tokens = near.shape[1]
    shapes = [(tokens, features)] * 3 + [(slot_rows, features), (out_rows, features)]
    return pl.pallas_call(
        final_kernel,
        in_specs=any_specs(2),
        out_shape=[jax.ShapeDtypeStruct(shape, BF) for shape in shapes],
        scratch_shapes=[
            pltpu.VMEM(arrived.shape, BF),
            pltpu.VMEM((ROW, tokens // 2, LANES), BF),
            pltpu.SemaphoreType.DMA((2,)),
        ],
        compiler_params=pltpu.CompilerParams(vmem_limit_bytes=16 << 20),
    )(arrived, near)


def shifted(block, distance):
    count = lax.axis_size("ctx")
    return lax.ppermute(block, "ctx", [(i, (i + distance) % count) for i in range(count)])


def swapped(block, bit):
    return lax.ppermute(block, "head", [(i, i ^ bit) for i in range(lax.axis_size("head"))])


def in_row(block):
    count = lax.axis_size("ctx")
    groups = [list(range(r, r + ROW)) for r in range(0, count, ROW)]
    return lax.all_to_all(block, "ctx", 0, 0, axis_index_groups=groups)


def in_column(block):
    count = lax.axis_size("ctx")
    groups = [list(range(x, count, ROW)) for x in range(ROW)]
    return lax.all_to_all(block, "ctx", 0, 0, axis_index_groups=groups)


def masked(block, mask):
    return lax.ppermute(block, "ctx", [(i, i ^ mask) for i in range(lax.axis_size("ctx"))])


def body(
    query, key, value, pos_store, owner, block_mask, content_bias, pos_bias, out_weight, d_layer
):
    tokens, features = query.shape
    slot_count = owner.shape[0]
    slot_rows = pos_store.shape[0]
    half = tokens // 2
    across = swapped(d_layer, 2)
    row = in_row(pack_call(block_mask, query, key, value, pos_store))
    halo = shifted(row[1:, :tokens], ROW)
    at = tokens + half
    pos = row[:, at : at + slot_rows // 2]
    far_pos = [pos] + [masked(pos, ROW * 4 * j) for j in range(1, 4)]
    far_pos = jnp.stack(far_pos)
    slots = [far_pos] + [masked(far_pos, ROW * j) for j in range(1, 4)]
    grads = [d_layer, swapped(d_layer, 1), across, swapped(across, 1)]
    ga = in_row(mix_call(grads, out_weight))
    near, own, far, dpos = core_call(
        owner, row, halo, slots, ga, content_bias[None], pos_bias[None]
    )
    back = shifted(far, -ROW)
    near = in_row(near)
    near, back = lax.optimization_barrier((near, back))
    sums = weight_call(near, grads, dpos)
    parts = in_column(sums.reshape((slot_count // ROW, ROW) + sums.shape[1:]))
    arrived = in_row(meet_call(own, back, parts))
    grad_query, grad_key, grad_value, grad_pos, grad_weight = final_call(
        arrived, near, features, slot_rows, slot_rows // 2
    )
    return grad_query, grad_key, grad_value, grad_pos, grad_weight.T


def solution(mesh):
    spread = P("ctx", "head")
    return jax.shard_map(
        body,
        mesh=mesh,
        in_specs=(
            spread, spread, spread, spread, P(), P("ctx", None), P("head"), P("head"),
            P("head", None), spread,
        ),
        out_specs=(spread, spread, spread, spread, P("head", "ctx")),
        check_vma=False,
    )
```

```python
import functools

import jax
import jax.numpy as jnp
from jax import lax
from jax.experimental import pallas as pl
from jax.experimental.pallas import tpu as pltpu
from jax.sharding import PartitionSpec as P

HD = 64
LANES = 128
NEG = -1e30
ROW = 4
BF = jnp.bfloat16
F32 = jnp.float32


def nt(a, b):
    return lax.dot_general(a, b, (((1,), (1,)), ((), ())), preferred_element_type=F32)


def nn(a, b):
    return lax.dot_general(a, b, (((1,), (0,)), ((), ())), preferred_element_type=F32)


def tn(a, b):
    return lax.dot_general(a, b, (((0,), (0,)), ((), ())), preferred_element_type=F32)


def lanes():
    return lax.broadcasted_iota(jnp.int32, (1, LANES), 1)


def turned(block, shift=HD):
    return pltpu.roll(block.astype(F32), shift, 1)


def joined(low, high):
    return jnp.where(lanes() < HD, low.astype(F32), high.astype(F32))


def of_head(array, head):
    pair = array[:, head // 2 * LANES : (head // 2 + 1) * LANES]
    return turned(pair) if head % 2 else pair.astype(F32)


def halves(array, head):
    both = of_head(array, head)
    middle = both.shape[0] // 2
    return joined(both[:middle], turned(both[middle:]))


def whole_of(first, second):
    top = joined(first, turned(second))
    bottom = joined(turned(first), second)
    return jnp.concatenate([top, bottom], axis=0)


def anti_diagonal(size):
    row = lax.broadcasted_iota(jnp.int32, (size, size), 0)
    col = lax.broadcasted_iota(jnp.int32, (size, size), 1)
    return (row + col == size - 1).astype(F32).astype(BF)


def vmem_specs(count):
    return [pl.BlockSpec(memory_space=pltpu.VMEM)] * count


def smem_specs(count):
    return [pl.BlockSpec(memory_space=pltpu.SMEM)] * count


def any_specs(count):
    return [pl.BlockSpec(memory_space=pl.ANY)] * count


def hbm_specs(count):
    return [pl.BlockSpec(memory_space=pltpu.HBM)] * count


def whole_spec(shape):
    return pl.BlockSpec(shape, lambda *_: (0,) * len(shape))


def brought(pairs, sems):
    copies = [
        pltpu.make_async_copy(source, target, sems.at[i])
        for i, (source, target) in enumerate(pairs)
    ]
    for copy in copies:
        copy.start()
    for copy in copies:
        copy.wait()


def pack_kernel(mask_ref, q_in, k_in, v_in, out_ref, q_ref, k_ref, v_ref, sems):
    brought([(q_in, q_ref), (k_in, k_ref), (v_in, v_ref)], sems)
    tokens = q_ref.shape[0]
    half = tokens // 2
    flags = jnp.zeros((16, LANES), F32)
    for lag in range(mask_ref.shape[1]):
        flags = jnp.where(lanes() == lag, mask_ref[0, lag].astype(F32), flags)
    for h in range(ROW):
        out_ref[h, :tokens, :] = joined(of_head(k_ref, h), turned(of_head(v_ref, h))).astype(BF)
        out_ref[h, tokens : tokens + half, :] = halves(q_ref, h).astype(BF)
        out_ref[h, tokens + half :, :] = flags.astype(BF)


def pack_call(mask, q, k, v):
    tokens = q.shape[0]
    rows = tokens + tokens // 2 + 16
    return pl.pallas_call(
        pack_kernel,
        in_specs=smem_specs(1) + hbm_specs(3),
        out_shape=pltpu.HBM((ROW, rows, LANES), BF),
        scratch_shapes=[pltpu.VMEM(a.shape, BF) for a in (q, k, v)]
        + [pltpu.SemaphoreType.DMA((3,))],
        compiler_params=pltpu.CompilerParams(vmem_limit_bytes=60 << 20),
    )(mask, q, k, v)


def mix_kernel(
    g0_in, g1_in, g2_in, g3_in, weight_in, s0_in, s1_in, s2_in, s3_in, out_ref,
    g0, g1, g2, g3, weight_ref, pos_ref, sems,
):
    rows = s0_in.shape[0]
    pairs = [(g0_in, g0), (g1_in, g1), (g2_in, g2), (g3_in, g3), (weight_in, weight_ref)]
    for i, part in enumerate((s0_in, s1_in, s2_in, s3_in)):
        pairs.append((part, pos_ref.at[i * rows : (i + 1) * rows]))
    brought(pairs, sems)
    tokens, features = g0.shape
    mixed = None
    for b, grad in enumerate((g0, g1, g2, g3)):
        at = pl.multiple_of((lax.axis_index("head") ^ b) * features, features)
        part = nt(grad[...], weight_ref[:, pl.ds(at, features)])
        mixed = part if mixed is None else mixed + part
    mixed = mixed.astype(BF)
    for h in range(ROW):
        out_ref[h, : tokens // 2, :] = halves(mixed, h).astype(BF)
        out_ref[h, tokens // 2 :, :] = halves(pos_ref, h).astype(BF)


def mix_call(grads, out_weight, slots):
    tokens, features = grads[0].shape
    rows = 4 * slots[0].shape[0]
    return pl.pallas_call(
        mix_kernel,
        in_specs=any_specs(9),
        out_shape=pltpu.HBM((ROW, (tokens + rows) // 2, LANES), BF),
        scratch_shapes=[pltpu.VMEM(a.shape, BF) for a in (*grads, out_weight)]
        + [pltpu.VMEM((rows, features), BF), pltpu.SemaphoreType.DMA((9,))],
        compiler_params=pltpu.CompilerParams(vmem_limit_bytes=16 << 20),
    )(*grads, out_weight, *slots)


def key_pairs(row_in, halo_in, keys, query, tokens):
    pairs = [(halo_in.at[b], keys.at[b * tokens : (b + 1) * tokens]) for b in range(ROW - 1)]
    for b in range(ROW):
        at = (ROW - 1 + b) * tokens
        pairs.append((row_in.at[b, 0:tokens], keys.at[at : at + tokens]))
        pairs.append((row_in.at[b, tokens : tokens + tokens // 2], query.at[b]))
    return pairs


def core_kernel(
    owner_ref, row_in, halo_in, ga_in, cb_in, pb_in,
    near_ref, own_ref, far_ref,
    keys, queries, pos_ref, ga_ref, dist_out, table, flipped, grads, dist,
    score_ref, rel_ref, low_ref, ds_ref, spread_ref, dot_ref, flag_ref, cb_ref, pb_ref, sems,
):
    tokens = halo_in.shape[1]
    half = tokens // 2
    span = ROW * tokens
    wide = span + half
    block = pl.program_id(0)
    anti = anti_diagonal(half)

    @pl.when(block == 0)
    def _():
        pairs = key_pairs(row_in, halo_in, keys, queries, tokens)
        count = owner_ref.shape[0]
        packed = pos_ref.shape[2]
        rows = 2 * packed * ROW // count
        pairs += [(ga_in.at[:, 0:half], ga_ref), (ga_in.at[:, half : half + packed], pos_ref.at[0])]
        pairs.append((row_in.at[:, tokens + half : tokens + half + 16], flag_ref))
        brought(pairs, sems)
        for b in range(ROW):
            pos_ref[1, b] = turned(pos_ref[0, b]).astype(BF)
        turn = (ROW - (lax.axis_index("ctx") & 3)) * HD % cb_in.shape[1]
        for bias_in, bias_ref in ((cb_in, cb_ref), (pb_in, pb_ref)):
            bias = jnp.broadcast_to(bias_in[...], (8, bias_in.shape[1]))
            bias_ref[...] = pltpu.roll(bias, turn, 1)[0:1, :LANES]
        grads[...] = jnp.zeros_like(grads)
        dist[...] = jnp.zeros_like(dist)
        table[0:tokens, :] = jnp.zeros((tokens, LANES), BF)
        for d in range(count):
            slot = owner_ref[d]
            apart = (slot >> 2) ^ (lax.axis_index("ctx") >> 2)
            place = (apart & 3) * 4 + (apart >> 2)
            at = pl.multiple_of((place & 7) * rows, rows)
            both = pos_ref[place >> 3, slot & 3, pl.ds(at, rows), :]
            table[tokens + d * rows : tokens + (d + 1) * rows, :] = both
        parts = (tokens + span) // half
        for i in range(parts):
            flipped[(parts - 1 - i) * half : (parts - i) * half, :] = nn(
                anti, table[i * half : (i + 1) * half, :]
            ).astype(BF)

    lane = lanes()
    low = lane < HD
    scale = jnp.asarray(0.125, BF)
    starts = [pl.multiple_of((block + w) * tokens, tokens) for w in range(ROW)]
    kept = []
    dqs = []
    chunk = 16
    groups = [slice(c, c + chunk) for c in range(0, half, chunk)]
    barred = []
    for lag in range(ROW - 1, 0, -1):
        there = (lax.axis_index("ctx") & ~3) + block >= lag
        flag = flag_ref[block, 0:1, lag : lag + 1].astype(F32)
        barred.append(jnp.where(there & (flag > 0.5), 0.0, NEG))
    state = [{}, {}]

    def first(r):
        query = queries[block].astype(F32)
        ga = ga_ref[block].astype(F32)
        query = turned(query) if r == 1 else query
        ga = turned(ga) if r == 0 else ga
        ga = jnp.where(low, 0.0, ga)
        cq = jnp.where(low, query + cb_ref[...], 0.0).astype(BF)
        pq = jnp.where(low, query + pb_ref[...], 0.0).astype(BF)
        state[r].update(ga=ga, gal=ga.astype(BF), cq=cq, pq=pq)
        base = half * (1 - r)
        rel_ref[r] = nt(pq * scale, flipped[base : base + wide, :])
        cqs = cq * scale
        for w in range(ROW):
            score_ref[r, :, w * tokens : (w + 1) * tokens] = nt(
                cqs, keys[pl.ds(starts[w], tokens), :]
            )

    def soften(r):
        for g in groups:
            moved = pltpu.roll(
                rel_ref[r, g, :], (span + 1 + g.start) % wide, 1, stride=1, stride_axis=0
            )
            scores = []
            for w in range(ROW):
                cols = slice(w * tokens, (w + 1) * tokens)
                s = score_ref[r, g, cols] + moved[:, cols]
                if w == ROW - 1:
                    row = lax.broadcasted_iota(jnp.int32, (chunk, tokens), 0) + r * half + g.start
                    col = lax.broadcasted_iota(jnp.int32, (chunk, tokens), 1)
                    s = jnp.where(col <= row, s, NEG)
                else:
                    s = s + barred[w]
                scores.append(s)
            top = functools.reduce(jnp.maximum, scores)
            top = jnp.max(top, axis=1, keepdims=True)
            weights = [jnp.exp(s - top) for s in scores]
            total = functools.reduce(jnp.add, weights)
            inv = 1.0 / jnp.sum(total, axis=1, keepdims=True)
            for w in range(ROW):
                cols = slice(w * tokens, (w + 1) * tokens)
                p = weights[w] * inv
                score_ref[r, g, cols] = p
                low_ref[r, g, cols] = p.astype(BF)

    def second(r):
        att = None
        for w in range(ROW):
            cols = slice(w * tokens, (w + 1) * tokens)
            part = nn(low_ref[r, :, cols], keys[pl.ds(starts[w], tokens), :])
            att = part if att is None else att + part
        att = att.astype(BF).astype(F32)
        state[r]["att"] = turned(att) if r == 0 else att
        dot = jnp.sum(state[r]["ga"] * att, axis=1, keepdims=True)
        dot_ref[r] = jnp.broadcast_to(dot, (half, LANES))
        for w in range(ROW):
            cols = slice(w * tokens, (w + 1) * tokens)
            rel_ref[r, :, cols] = nt(state[r]["gal"], keys[pl.ds(starts[w], tokens), :])

    def steepen(r):
        for g in groups:
            dot = dot_ref[r, g, 0:1]
            for w in range(ROW):
                cols = slice(w * tokens, (w + 1) * tokens)
                ds = 0.125 * score_ref[r, g, cols] * (rel_ref[r, g, cols] - dot)
                ds_ref[r, g, cols] = ds.astype(BF)

    def third(r):
        acc = None
        for w in range(ROW):
            cols = slice(w * tokens, (w + 1) * tokens)
            ds = ds_ref[r, :, cols]
            for x in range(2):
                at = (2 * ROW - 1 - (2 * w + x)) * half
                rel_ref[r, :, at : at + half] = nn(ds[:, x * half : (x + 1) * half], anti)
        rel_ref[r, :, span:] = jnp.zeros((half, wide - span), F32)
        for w in range(ROW):
            cols = slice(w * tokens, (w + 1) * tokens)
            ds = ds_ref[r, :, cols]
            grads[:, pl.ds(starts[w], tokens)] += tn(state[r]["cq"], ds) + tn(
                state[r]["gal"], low_ref[r, :, cols]
            )
            part = nn(ds, keys[pl.ds(starts[w], tokens), :])
            acc = part if acc is None else acc + part
        state[r]["acc"] = acc

    def slant(r):
        for g in groups:
            spread_ref[r, g, :] = pltpu.roll(
                rel_ref[r, g, :], 1 + g.start, 1, stride=1, stride_axis=0
            ).astype(BF)

    def fourth(r):
        start = half * r
        acc = state[r]["acc"] + nn(spread_ref[r], table[start : start + wide, :])
        dist[:, start : start + wide] += tn(state[r]["pq"], spread_ref[r])
        state[r]["acc"] = turned(acc) if r == 1 else acc

    first(0)
    for stage, other in (
        (soften, first), (second, soften), (steepen, second), (third, steepen), (slant, third),
        (fourth, slant),
    ):
        stage(0)
        other(1)
    fourth(1)
    kept = [part["att"] for part in state]
    dqs = [part["acc"] for part in state]
    near_ref[block, :half, :] = joined(kept[0], kept[1]).astype(BF)
    near_ref[block, half:tokens, :] = joined(dqs[0], dqs[1]).astype(BF)

    @pl.when(block == ROW - 1)
    def _():
        for b in range(ROW - 1):
            far_ref[b] = grads[:, b * tokens : (b + 1) * tokens].T.astype(BF)
        for b in range(ROW):
            at = (ROW - 1 + b) * tokens
            own_ref[b] = grads[:, at : at + tokens].T
        count = owner_ref.shape[0]
        packed = pos_ref.shape[2]
        rows = 2 * packed * ROW // count
        dist_out[...] = dist[:, tokens:].T
        for d in range(count):
            slot = owner_ref[d]
            part = dist_out[d * rows : (d + 1) * rows, :].astype(BF)
            place = slot >> 2
            at = pl.multiple_of((place & 7) * rows, rows)
            pos_ref[place >> 3, slot & 3, pl.ds(at, rows), :] = part
        for b in range(ROW):
            near_ref[b, tokens:, :] = joined(pos_ref[0, b], turned(pos_ref[1, b])).astype(BF)


def core_call(owner, row, halo, ga, cb, pb):
    tokens = halo.shape[1]
    half = tokens // 2
    packed = ga.shape[1] - half
    rel = ROW * packed * 2
    shapes = [
        ((ROW, tokens + packed, LANES), BF), ((ROW, tokens, LANES), F32),
        ((ROW - 1, tokens, LANES), BF),
    ]
    return pl.pallas_call(
        core_kernel,
        grid=(ROW,),
        in_specs=smem_specs(1) + any_specs(3) + vmem_specs(2),
        out_specs=[whole_spec(shape) for shape, _ in shapes],
        out_shape=[pltpu.HBM(shape, dtype) for shape, dtype in shapes],
        scratch_shapes=[
            pltpu.VMEM(((2 * ROW - 1) * tokens, LANES), BF),
            pltpu.VMEM((ROW, half, LANES), BF),
            pltpu.VMEM((2, ROW, packed, LANES), BF),
            pltpu.VMEM((ROW, half, LANES), BF),
            pltpu.VMEM((rel, LANES), F32),
            pltpu.VMEM((tokens + rel, LANES), BF),
            pltpu.VMEM((tokens + rel, LANES), BF),
            pltpu.VMEM((LANES, (2 * ROW - 1) * tokens), F32),
            pltpu.VMEM((LANES, tokens + rel), F32),
            pltpu.VMEM((2, half, ROW * tokens), F32),
            pltpu.VMEM((2, half, ROW * tokens + half), F32),
            pltpu.VMEM((2, half, ROW * tokens), BF),
            pltpu.VMEM((2, half, ROW * tokens), BF),
            pltpu.VMEM((2, half, ROW * tokens + half), BF),
            pltpu.VMEM((2, half, LANES), F32),
            pltpu.VMEM((ROW, 16, LANES), BF),
            pltpu.VMEM((1, LANES), F32),
            pltpu.VMEM((1, LANES), F32),
            pltpu.SemaphoreType.DMA((3 * ROW + 2,)),
        ],
        compiler_params=pltpu.CompilerParams(vmem_limit_bytes=60 << 20),
        cost_estimate=pl.CostEstimate(
            flops=40_000_000_000, bytes_accessed=8_000_000, transcendentals=0
        ),
    )(owner, row, halo, ga, cb, pb)


def weight_kernel(
    att_in, g0_in, g1_in, g2_in, g3_in, own_in, far_in, out_ref,
    att_ref, g0, g1, g2, g3, own_ref, far_ref, sems,
):
    half = att_ref.shape[1]
    tokens, features = g0.shape
    sources = [att_in.at[:, 0:half], g0_in, g1_in, g2_in, g3_in, own_in, far_in]
    brought(zip(sources, [att_ref, g0, g1, g2, g3, own_ref, far_ref]), sems)
    for b in range(ROW):
        grad = own_ref[b]
        if b > 0:
            grad = grad + far_ref[b - 1].astype(F32)
        out_ref[b, :tokens, :] = grad.astype(BF)
    rows = 16
    chunks = features // rows
    column = 4 * features // (ROW * rows)
    for pair in range(features // LANES):
        att = whole_of(att_ref[2 * pair], att_ref[2 * pair + 1]).astype(BF)
        for b, grad in enumerate((g0, g1, g2, g3)):
            term = tn(att, grad[...]).T.astype(BF)
            first = (lax.axis_index("head") ^ b) * (chunks // ROW)
            for c in range(chunks):
                at = tokens + (pair * column + first + c // ROW) * rows
                out_ref[c % ROW, pl.ds(pl.multiple_of(at, rows), rows), :] = term[
                    c * rows : (c + 1) * rows
                ]


def weight_call(near, grads, own, far):
    tokens, features = grads[0].shape
    rows = tokens + 4 * features // ROW * (features // LANES)
    return pl.pallas_call(
        weight_kernel,
        in_specs=any_specs(7),
        out_shape=pltpu.HBM((ROW, rows, LANES), BF),
        scratch_shapes=[pltpu.VMEM((ROW, tokens // 2, LANES), BF)]
        + [pltpu.VMEM(a.shape, a.dtype) for a in (*grads, own, far)]
        + [pltpu.SemaphoreType.DMA((7,))],
        compiler_params=pltpu.CompilerParams(vmem_limit_bytes=16 << 20),
    )(near, *grads, own, far)


def sum_kernel(row_in, near_in, out_ref, row_ref, near_ref, sems):
    column, rows, features = out_ref.shape
    weight_rows = 16
    pos_rows = rows - weight_rows
    tokens = row_in.shape[1] - column * weight_rows * (features // LANES)
    near_rows = near_in.shape[1]
    sources = [row_in.at[:, tokens:], near_in.at[:, tokens:near_rows]]
    brought(zip(sources, [row_ref, near_ref]), sems)
    for pair in range(features // LANES):
        cols = slice(pair * LANES, (pair + 1) * LANES)
        pos = whole_of(near_ref[2 * pair], near_ref[2 * pair + 1]).astype(BF)
        part = slice(pair * column * weight_rows, (pair + 1) * column * weight_rows)
        total = row_ref[0, part, :].astype(F32)
        for x in range(1, ROW):
            total = total + row_ref[x, part, :].astype(F32)
        total = total.astype(BF)
        for z in range(column):
            out_ref[z, :pos_rows, cols] = pos[z * pos_rows : (z + 1) * pos_rows]
            out_ref[z, pos_rows:, cols] = total[z * weight_rows : (z + 1) * weight_rows]


def sum_call(row, near, column, pos_rows, features, tokens):
    return pl.pallas_call(
        sum_kernel,
        in_specs=any_specs(2),
        out_shape=pltpu.HBM((column, pos_rows + 16, features), BF),
        scratch_shapes=[
            pltpu.VMEM((ROW, row.shape[1] - tokens, LANES), BF),
            pltpu.VMEM((ROW, near.shape[1] - tokens, LANES), BF),
            pltpu.SemaphoreType.DMA((2,)),
        ],
        compiler_params=pltpu.CompilerParams(vmem_limit_bytes=16 << 20),
    )(row, near)


def grads_kernel(row_in, near_in, dq_ref, dk_ref, dv_ref, row_ref, near_ref, sems):
    tokens = dq_ref.shape[0]
    sources = [row_in.at[:, 0:tokens], near_in.at[:, tokens // 2 : tokens]]
    brought(zip(sources, [row_ref, near_ref]), sems)
    for pair in range(ROW // 2):
        cols = slice(pair * LANES, (pair + 1) * LANES)
        dq_ref[:, cols] = whole_of(near_ref[2 * pair], near_ref[2 * pair + 1]).astype(BF)
        a, b = row_ref[2 * pair], row_ref[2 * pair + 1]
        dk_ref[:, cols] = joined(a, turned(b)).astype(BF)
        dv_ref[:, cols] = joined(turned(a), b).astype(BF)


def grads_call(row, near, tokens, features):
    return pl.pallas_call(
        grads_kernel,
        in_specs=any_specs(2),
        out_shape=[jax.ShapeDtypeStruct((tokens, features), BF)] * 3,
        scratch_shapes=[
            pltpu.VMEM((ROW, tokens, LANES), BF),
            pltpu.VMEM((ROW, tokens // 2, LANES), BF),
            pltpu.SemaphoreType.DMA((2,)),
        ],
        compiler_params=pltpu.CompilerParams(vmem_limit_bytes=16 << 20),
    )(row, near)


def final_kernel(parts_in, dpos_ref, dw_ref, parts_ref, sems):
    brought([(parts_in, parts_ref)], sems)
    cut = dpos_ref.shape[0]
    total = parts_ref[0].astype(F32)
    for z in range(1, parts_ref.shape[0]):
        total = total + parts_ref[z].astype(F32)
    dpos_ref[...] = total[:cut].astype(BF)
    dw_ref[...] = total[cut:].astype(BF)


def final_call(parts, pos_rows):
    rows, features = parts.shape[1:]
    shapes = [(pos_rows, features), (rows - pos_rows, features)]
    return pl.pallas_call(
        final_kernel,
        in_specs=any_specs(1),
        out_shape=[jax.ShapeDtypeStruct(shape, BF) for shape in shapes],
        scratch_shapes=[pltpu.VMEM(parts.shape, BF), pltpu.SemaphoreType.DMA((1,))],
        compiler_params=pltpu.CompilerParams(vmem_limit_bytes=16 << 20),
    )(parts)


def shifted(block, distance):
    count = lax.axis_size("ctx")
    return lax.ppermute(block, "ctx", [(i, (i + distance) % count) for i in range(count)])


def swapped(block, bit):
    return lax.ppermute(block, "head", [(i, i ^ bit) for i in range(lax.axis_size("head"))])


def in_row(block):
    count = lax.axis_size("ctx")
    groups = [list(range(r, r + ROW)) for r in range(0, count, ROW)]
    return lax.all_to_all(block, "ctx", 0, 0, axis_index_groups=groups)


def in_column(block):
    count = lax.axis_size("ctx")
    groups = [list(range(x, count, ROW)) for x in range(ROW)]
    return lax.all_to_all(block, "ctx", 0, 0, axis_index_groups=groups)


def masked(block, mask):
    return lax.ppermute(block, "ctx", [(i, i ^ mask) for i in range(lax.axis_size("ctx"))])


def body(
    query, key, value, pos_store, owner, block_mask, content_bias, pos_bias, out_weight, d_layer
):
    tokens, features = query.shape
    slot_count = owner.shape[0]
    slot_rows = pos_store.shape[0]
    column = slot_count // ROW
    across = swapped(d_layer, 2)
    far_pos = [pos_store] + [masked(pos_store, ROW * 4 * j) for j in range(1, 4)]
    packed = pack_call(block_mask, query, key, value)
    packed, across, *far_pos = lax.optimization_barrier((packed, across, *far_pos))
    far_pos = jnp.concatenate(far_pos, axis=0)
    slots = [far_pos] + [masked(far_pos, ROW * j) for j in range(1, 4)]
    row = in_row(packed)
    halo = shifted(row[1:, :tokens], ROW)
    grads = [d_layer, swapped(d_layer, 1), across, swapped(across, 1)]
    ga = in_row(mix_call(grads, out_weight, slots))
    near, own, far = core_call(owner, row, halo, ga, content_bias[None], pos_bias[None])
    back = shifted(far, -ROW)
    near = in_row(near)
    near, back = lax.optimization_barrier((near, back))
    met = in_row(weight_call(near, grads, own, back))
    parts = in_column(sum_call(met, near, column, slot_rows, features, tokens))
    grad_query, grad_key, grad_value = grads_call(met, near, tokens, features)
    grad_pos, grad_weight = final_call(parts, slot_rows)
    return grad_query, grad_key, grad_value, grad_pos, grad_weight.T


def solution(mesh):
    spread = P("ctx", "head")
    return jax.shard_map(
        body,
        mesh=mesh,
        in_specs=(
            spread, spread, spread, spread, P(), P("ctx", None), P("head"), P("head"),
            P("head", None), spread,
        ),
        out_specs=(spread, spread, spread, spread, P("head", "ctx")),
        check_vma=False,
    )
```

```python
import functools

import jax
import jax.numpy as jnp
from jax import lax
from jax.experimental import pallas as pl
from jax.experimental.pallas import tpu as pltpu
from jax.sharding import PartitionSpec as P

HD = 64
LANES = 128
NEG = -1e30
ROW = 4
BF = jnp.bfloat16
F32 = jnp.float32


def nt(a, b):
    return lax.dot_general(a, b, (((1,), (1,)), ((), ())), preferred_element_type=F32)


def nn(a, b):
    return lax.dot_general(a, b, (((1,), (0,)), ((), ())), preferred_element_type=F32)


def tn(a, b):
    return lax.dot_general(a, b, (((0,), (0,)), ((), ())), preferred_element_type=F32)


def lanes():
    return lax.broadcasted_iota(jnp.int32, (1, LANES), 1)


def turned(block, shift=HD):
    return pltpu.roll(block.astype(F32), shift, 1)


def joined(low, high):
    return jnp.where(lanes() < HD, low.astype(F32), high.astype(F32))


def of_head(array, head):
    pair = array[:, head // 2 * LANES : (head // 2 + 1) * LANES]
    return turned(pair) if head % 2 else pair.astype(F32)


def halves(array, head):
    both = of_head(array, head)
    middle = both.shape[0] // 2
    return joined(both[:middle], turned(both[middle:]))


def whole_of(first, second):
    top = joined(first, turned(second))
    bottom = joined(turned(first), second)
    return jnp.concatenate([top, bottom], axis=0)


def anti_diagonal(size):
    row = lax.broadcasted_iota(jnp.int32, (size, size), 0)
    col = lax.broadcasted_iota(jnp.int32, (size, size), 1)
    return (row + col == size - 1).astype(F32).astype(BF)


def vmem_specs(count):
    return [pl.BlockSpec(memory_space=pltpu.VMEM)] * count


def smem_specs(count):
    return [pl.BlockSpec(memory_space=pltpu.SMEM)] * count


def any_specs(count):
    return [pl.BlockSpec(memory_space=pl.ANY)] * count


def hbm_specs(count):
    return [pl.BlockSpec(memory_space=pltpu.HBM)] * count


def whole_spec(shape):
    return pl.BlockSpec(shape, lambda *_: (0,) * len(shape))


def brought(pairs, sems, meanwhile=lambda: None):
    copies = [
        pltpu.make_async_copy(source, target, sems.at[i])
        for i, (source, target) in enumerate(pairs)
    ]
    for copy in copies:
        copy.start()
    meanwhile()
    for copy in copies:
        copy.wait()


def pack_kernel(mask_ref, q_in, k_in, v_in, out_ref, q_ref, k_ref, v_ref, sems):
    brought([(q_in, q_ref), (k_in, k_ref), (v_in, v_ref)], sems)
    tokens = q_ref.shape[0]
    half = tokens // 2
    flags = jnp.zeros((16, LANES), F32)
    for lag in range(mask_ref.shape[1]):
        flags = jnp.where(lanes() == lag, mask_ref[0, lag].astype(F32), flags)
    for h in range(ROW):
        out_ref[h, :tokens, :] = joined(of_head(k_ref, h), turned(of_head(v_ref, h))).astype(BF)
        out_ref[h, tokens : tokens + half, :] = halves(q_ref, h).astype(BF)
        out_ref[h, tokens + half :, :] = flags.astype(BF)


def pack_call(mask, q, k, v):
    tokens = q.shape[0]
    rows = tokens + tokens // 2 + 16
    return pl.pallas_call(
        pack_kernel,
        in_specs=smem_specs(1) + hbm_specs(3),
        out_shape=pltpu.HBM((ROW, rows, LANES), BF),
        scratch_shapes=[pltpu.VMEM(a.shape, BF) for a in (q, k, v)]
        + [pltpu.SemaphoreType.DMA((3,))],
        compiler_params=pltpu.CompilerParams(vmem_limit_bytes=60 << 20),
    )(mask, q, k, v)


def mix_kernel(
    g0_in, g1_in, g2_in, g3_in, weight_in, s0_in, s1_in, s2_in, s3_in, out_ref,
    g0, g1, g2, g3, weight_ref, pos_ref, sems,
):
    rows = s0_in.shape[0]
    pairs = [(g0_in, g0), (g1_in, g1), (g2_in, g2), (g3_in, g3), (weight_in, weight_ref)]
    for i, part in enumerate((s0_in, s1_in, s2_in, s3_in)):
        pairs.append((part, pos_ref.at[i * rows : (i + 1) * rows]))
    brought(pairs, sems)
    tokens, features = g0.shape
    mixed = None
    for b, grad in enumerate((g0, g1, g2, g3)):
        at = pl.multiple_of((lax.axis_index("head") ^ b) * features, features)
        part = nt(grad[...], weight_ref[:, pl.ds(at, features)])
        mixed = part if mixed is None else mixed + part
    mixed = mixed.astype(BF)
    for h in range(ROW):
        out_ref[h, : tokens // 2, :] = halves(mixed, h).astype(BF)
        out_ref[h, tokens // 2 :, :] = halves(pos_ref, h).astype(BF)


def mix_call(grads, out_weight, slots):
    tokens, features = grads[0].shape
    rows = 4 * slots[0].shape[0]
    return pl.pallas_call(
        mix_kernel,
        in_specs=any_specs(9),
        out_shape=pltpu.HBM((ROW, (tokens + rows) // 2, LANES), BF),
        scratch_shapes=[pltpu.VMEM(a.shape, BF) for a in (*grads, out_weight)]
        + [pltpu.VMEM((rows, features), BF), pltpu.SemaphoreType.DMA((9,))],
        compiler_params=pltpu.CompilerParams(vmem_limit_bytes=16 << 20),
    )(*grads, out_weight, *slots)


def key_pairs(row_in, halo_in, keys, query, tokens):
    pairs = [(halo_in.at[b], keys.at[b * tokens : (b + 1) * tokens]) for b in range(ROW - 1)]
    for b in range(ROW):
        at = (ROW - 1 + b) * tokens
        pairs.append((row_in.at[b, 0:tokens], keys.at[at : at + tokens]))
        pairs.append((row_in.at[b, tokens : tokens + tokens // 2], query.at[b]))
    return pairs


def core_kernel(
    owner_ref, row_in, halo_in, ga_in, cb_in, pb_in,
    near_ref, own_ref, far_ref,
    keys, queries, pos_ref, ga_ref, dist_out, table, flipped, grads, dist,
    score_ref, rel_ref, low_ref, ds_ref, spread_ref, dot_ref, flag_ref, cb_ref, pb_ref, sems,
):
    tokens = halo_in.shape[1]
    half = tokens // 2
    span = ROW * tokens
    wide = span + half
    block = pl.program_id(0)
    anti = anti_diagonal(half)

    @pl.when(block == 0)
    def _():
        pairs = key_pairs(row_in, halo_in, keys, queries, tokens)
        count = owner_ref.shape[0]
        packed = pos_ref.shape[2]
        rows = 2 * packed * ROW // count
        pairs += [(ga_in.at[:, 0:half], ga_ref), (ga_in.at[:, half : half + packed], pos_ref.at[0])]
        pairs.append((row_in.at[:, tokens + half : tokens + half + 16], flag_ref))

        def clear():
            grads[...] = jnp.zeros_like(grads)
            dist[...] = jnp.zeros_like(dist)
            table[0:tokens, :] = jnp.zeros((tokens, LANES), BF)

        brought(pairs, sems, clear)
        for b in range(ROW):
            pos_ref[1, b] = turned(pos_ref[0, b]).astype(BF)
        turn = (ROW - (lax.axis_index("ctx") & 3)) * HD % cb_in.shape[1]
        for bias_in, bias_ref in ((cb_in, cb_ref), (pb_in, pb_ref)):
            bias = jnp.broadcast_to(bias_in[...], (8, bias_in.shape[1]))
            bias_ref[...] = pltpu.roll(bias, turn, 1)[0:1, :LANES]
        for d in range(count):
            slot = owner_ref[d]
            apart = (slot >> 2) ^ (lax.axis_index("ctx") >> 2)
            place = (apart & 3) * 4 + (apart >> 2)
            at = pl.multiple_of((place & 7) * rows, rows)
            both = pos_ref[place >> 3, slot & 3, pl.ds(at, rows), :]
            table[tokens + d * rows : tokens + (d + 1) * rows, :] = both
        parts = (tokens + span) // half
        for i in range(parts):
            flipped[(parts - 1 - i) * half : (parts - i) * half, :] = nn(
                anti, table[i * half : (i + 1) * half, :]
            ).astype(BF)

    lane = lanes()
    low = lane < HD
    scale = jnp.asarray(0.125, BF)
    starts = [pl.multiple_of((block + w) * tokens, tokens) for w in range(ROW)]
    kept = []
    dqs = []
    chunk = 16
    groups = [slice(c, c + chunk) for c in range(0, half, chunk)]
    barred = []
    for lag in range(ROW - 1, 0, -1):
        there = (lax.axis_index("ctx") & ~3) + block >= lag
        flag = flag_ref[block, 0:1, lag : lag + 1].astype(F32)
        barred.append(jnp.where(there & (flag > 0.5), 0.0, NEG))
    state = [{}, {}]

    def cols_of(w, r):
        width = half if r == 0 and w == ROW - 1 else tokens
        return width, slice(w * tokens, w * tokens + width)

    def first(r):
        query = queries[block].astype(F32)
        ga = ga_ref[block].astype(F32)
        query = turned(query) if r == 1 else query
        ga = turned(ga) if r == 0 else ga
        ga = jnp.where(low, 0.0, ga)
        cq = jnp.where(low, query + cb_ref[...], 0.0).astype(BF)
        pq = jnp.where(low, query + pb_ref[...], 0.0).astype(BF)
        state[r].update(ga=ga, gal=ga.astype(BF), cq=cq, pq=pq)
        base = half * (1 - r)
        width = span if r == 0 else wide
        rel_ref[r, :, :width] = nt(pq * scale, flipped[base : base + width, :])
        cqs = cq * scale
        for w in range(ROW):
            width, cols = cols_of(w, r)
            score_ref[r, :, cols] = nt(cqs, keys[pl.ds(starts[w], width), :])

    def soften(r):
        for g in groups:
            moved = pltpu.roll(
                rel_ref[r, g, :], (span + 1 + g.start) % wide, 1, stride=1, stride_axis=0
            )
            scores = []
            for w in range(ROW):
                width, cols = cols_of(w, r)
                s = score_ref[r, g, cols] + moved[:, cols]
                if w == ROW - 1:
                    row = lax.broadcasted_iota(jnp.int32, (chunk, width), 0) + r * half + g.start
                    col = lax.broadcasted_iota(jnp.int32, (chunk, width), 1)
                    s = jnp.where(col <= row, s, NEG)
                else:
                    s = s + barred[w]
                scores.append(s)
            parts = [s[:, x : x + half] for s in scores for x in range(0, s.shape[1], half)]
            top = functools.reduce(jnp.maximum, parts)
            top = jnp.max(top, axis=1, keepdims=True)
            weights = [jnp.exp(s - top) for s in scores]
            parts = [e[:, x : x + half] for e in weights for x in range(0, e.shape[1], half)]
            total = functools.reduce(jnp.add, parts)
            inv = 1.0 / jnp.sum(total, axis=1, keepdims=True)
            for w in range(ROW):
                _, cols = cols_of(w, r)
                p = weights[w] * inv
                score_ref[r, g, cols] = p
                low_ref[r, g, cols] = p.astype(BF)

    def second(r):
        att = None
        for w in range(ROW):
            width, cols = cols_of(w, r)
            part = nn(low_ref[r, :, cols], keys[pl.ds(starts[w], width), :])
            att = part if att is None else att + part
        att = att.astype(BF).astype(F32)
        state[r]["att"] = turned(att) if r == 0 else att
        dot = jnp.sum(state[r]["ga"] * att, axis=1, keepdims=True)
        dot_ref[r] = jnp.broadcast_to(dot, (half, LANES))
        for w in range(ROW):
            width, cols = cols_of(w, r)
            rel_ref[r, :, cols] = nt(state[r]["gal"], keys[pl.ds(starts[w], width), :])

    def steepen(r):
        for g in groups:
            dot = dot_ref[r, g, 0:1]
            for w in range(ROW):
                _, cols = cols_of(w, r)
                ds = 0.125 * score_ref[r, g, cols] * (rel_ref[r, g, cols] - dot)
                ds_ref[r, g, cols] = ds.astype(BF)

    def third(r):
        acc = None
        for w in range(ROW):
            width, cols = cols_of(w, r)
            ds = ds_ref[r, :, cols]
            for x in range(width // half):
                at = (2 * ROW - 1 - (2 * w + x)) * half
                rel_ref[r, :, at : at + half] = nn(ds[:, x * half : (x + 1) * half], anti)
        if r == 0:
            rel_ref[r, :, :half] = jnp.zeros((half, half), F32)
        rel_ref[r, :, span:] = jnp.zeros((half, wide - span), F32)
        for w in range(ROW):
            width, cols = cols_of(w, r)
            ds = ds_ref[r, :, cols]
            grads[:, pl.ds(starts[w], width)] += tn(state[r]["cq"], ds) + tn(
                state[r]["gal"], low_ref[r, :, cols]
            )
            part = nn(ds, keys[pl.ds(starts[w], width), :])
            acc = part if acc is None else acc + part
        state[r]["acc"] = acc

    def slant(r):
        for g in groups:
            spread_ref[r, g, :] = pltpu.roll(
                rel_ref[r, g, :], 1 + g.start, 1, stride=1, stride_axis=0
            ).astype(BF)

    def fourth(r):
        skip = half if r == 0 else 0
        start, stop = half * r + skip, half * r + wide
        spread = spread_ref[r, :, skip:]
        acc = state[r]["acc"] + nn(spread, table[start:stop, :])
        dist[:, start:stop] += tn(state[r]["pq"], spread)
        state[r]["acc"] = turned(acc) if r == 1 else acc

    first(0)
    for stage, other in (
        (soften, first), (second, soften), (steepen, second), (third, steepen), (slant, third),
        (fourth, slant),
    ):
        stage(0)
        other(1)
    fourth(1)
    kept = [part["att"] for part in state]
    dqs = [part["acc"] for part in state]
    near_ref[block, :half, :] = joined(kept[0], kept[1]).astype(BF)
    near_ref[block, half:tokens, :] = joined(dqs[0], dqs[1]).astype(BF)

    @pl.when(block == ROW - 1)
    def _():
        for b in range(ROW - 1):
            far_ref[b] = grads[:, b * tokens : (b + 1) * tokens].T.astype(BF)
        for b in range(ROW):
            at = (ROW - 1 + b) * tokens
            own_ref[b] = grads[:, at : at + tokens].T
        count = owner_ref.shape[0]
        packed = pos_ref.shape[2]
        rows = 2 * packed * ROW // count
        dist_out[...] = dist[:, tokens:].T
        for d in range(count):
            slot = owner_ref[d]
            part = dist_out[d * rows : (d + 1) * rows, :].astype(BF)
            place = slot >> 2
            at = pl.multiple_of((place & 7) * rows, rows)
            pos_ref[place >> 3, slot & 3, pl.ds(at, rows), :] = part
        for b in range(ROW):
            near_ref[b, tokens:, :] = joined(pos_ref[0, b], turned(pos_ref[1, b])).astype(BF)


def core_call(owner, row, halo, ga, cb, pb):
    tokens = halo.shape[1]
    half = tokens // 2
    packed = ga.shape[1] - half
    rel = ROW * packed * 2
    shapes = [
        ((ROW, tokens + packed, LANES), BF), ((ROW, tokens, LANES), F32),
        ((ROW - 1, tokens, LANES), BF),
    ]
    return pl.pallas_call(
        core_kernel,
        grid=(ROW,),
        in_specs=smem_specs(1) + any_specs(3) + vmem_specs(2),
        out_specs=[whole_spec(shape) for shape, _ in shapes],
        out_shape=[pltpu.HBM(shape, dtype) for shape, dtype in shapes],
        scratch_shapes=[
            pltpu.VMEM(((2 * ROW - 1) * tokens, LANES), BF),
            pltpu.VMEM((ROW, half, LANES), BF),
            pltpu.VMEM((2, ROW, packed, LANES), BF),
            pltpu.VMEM((ROW, half, LANES), BF),
            pltpu.VMEM((rel, LANES), F32),
            pltpu.VMEM((tokens + rel, LANES), BF),
            pltpu.VMEM((tokens + rel, LANES), BF),
            pltpu.VMEM((LANES, (2 * ROW - 1) * tokens), F32),
            pltpu.VMEM((LANES, tokens + rel), F32),
            pltpu.VMEM((2, half, ROW * tokens), F32),
            pltpu.VMEM((2, half, ROW * tokens + half), F32),
            pltpu.VMEM((2, half, ROW * tokens), BF),
            pltpu.VMEM((2, half, ROW * tokens), BF),
            pltpu.VMEM((2, half, ROW * tokens + half), BF),
            pltpu.VMEM((2, half, LANES), F32),
            pltpu.VMEM((ROW, 16, LANES), BF),
            pltpu.VMEM((1, LANES), F32),
            pltpu.VMEM((1, LANES), F32),
            pltpu.SemaphoreType.DMA((3 * ROW + 2,)),
        ],
        compiler_params=pltpu.CompilerParams(vmem_limit_bytes=60 << 20),
        cost_estimate=pl.CostEstimate(
            flops=40_000_000_000, bytes_accessed=8_000_000, transcendentals=0
        ),
    )(owner, row, halo, ga, cb, pb)


def weight_kernel(
    att_in, g0_in, g1_in, g2_in, g3_in, own_in, far_in, out_ref,
    att_ref, g0, g1, g2, g3, own_ref, far_ref, sems,
):
    half = att_ref.shape[1]
    tokens, features = g0.shape
    sources = [att_in.at[:, 0:half], g0_in, g1_in, g2_in, g3_in, own_in, far_in]
    brought(zip(sources, [att_ref, g0, g1, g2, g3, own_ref, far_ref]), sems)
    for b in range(ROW):
        grad = own_ref[b]
        if b > 0:
            grad = grad + far_ref[b - 1].astype(F32)
        out_ref[b, :tokens, :] = grad.astype(BF)
    rows = 16
    chunks = features // rows
    column = 4 * features // (ROW * rows)
    for pair in range(features // LANES):
        att = whole_of(att_ref[2 * pair], att_ref[2 * pair + 1]).astype(BF)
        for b, grad in enumerate((g0, g1, g2, g3)):
            term = tn(att, grad[...]).T.astype(BF)
            first = (lax.axis_index("head") ^ b) * (chunks // ROW)
            for c in range(chunks):
                at = tokens + (pair * column + first + c // ROW) * rows
                out_ref[c % ROW, pl.ds(pl.multiple_of(at, rows), rows), :] = term[
                    c * rows : (c + 1) * rows
                ]


def weight_call(near, grads, own, far):
    tokens, features = grads[0].shape
    rows = tokens + 4 * features // ROW * (features // LANES)
    return pl.pallas_call(
        weight_kernel,
        in_specs=any_specs(7),
        out_shape=pltpu.HBM((ROW, rows, LANES), BF),
        scratch_shapes=[pltpu.VMEM((ROW, tokens // 2, LANES), BF)]
        + [pltpu.VMEM(a.shape, a.dtype) for a in (*grads, own, far)]
        + [pltpu.SemaphoreType.DMA((7,))],
        compiler_params=pltpu.CompilerParams(vmem_limit_bytes=16 << 20),
    )(near, *grads, own, far)


def sum_kernel(row_in, near_in, out_ref, row_ref, near_ref, sems):
    column, rows, features = out_ref.shape
    weight_rows = 16
    pos_rows = rows - weight_rows
    tokens = row_in.shape[1] - column * weight_rows * (features // LANES)
    near_rows = near_in.shape[1]
    sources = [row_in.at[:, tokens:], near_in.at[:, tokens:near_rows]]
    brought(zip(sources, [row_ref, near_ref]), sems)
    for pair in range(features // LANES):
        cols = slice(pair * LANES, (pair + 1) * LANES)
        pos = whole_of(near_ref[2 * pair], near_ref[2 * pair + 1]).astype(BF)
        part = slice(pair * column * weight_rows, (pair + 1) * column * weight_rows)
        total = row_ref[0, part, :].astype(F32)
        for x in range(1, ROW):
            total = total + row_ref[x, part, :].astype(F32)
        total = total.astype(BF)
        for z in range(column):
            out_ref[z, :pos_rows, cols] = pos[z * pos_rows : (z + 1) * pos_rows]
            out_ref[z, pos_rows:, cols] = total[z * weight_rows : (z + 1) * weight_rows]


def sum_call(row, near, column, pos_rows, features, tokens):
    return pl.pallas_call(
        sum_kernel,
        in_specs=any_specs(2),
        out_shape=pltpu.HBM((column, pos_rows + 16, features), BF),
        scratch_shapes=[
            pltpu.VMEM((ROW, row.shape[1] - tokens, LANES), BF),
            pltpu.VMEM((ROW, near.shape[1] - tokens, LANES), BF),
            pltpu.SemaphoreType.DMA((2,)),
        ],
        compiler_params=pltpu.CompilerParams(vmem_limit_bytes=16 << 20),
    )(row, near)


def grads_kernel(row_in, near_in, dq_ref, dk_ref, dv_ref, row_ref, near_ref, sems):
    tokens = dq_ref.shape[0]
    sources = [row_in.at[:, 0:tokens], near_in.at[:, tokens // 2 : tokens]]
    brought(zip(sources, [row_ref, near_ref]), sems)
    for pair in range(ROW // 2):
        cols = slice(pair * LANES, (pair + 1) * LANES)
        dq_ref[:, cols] = whole_of(near_ref[2 * pair], near_ref[2 * pair + 1]).astype(BF)
        a, b = row_ref[2 * pair], row_ref[2 * pair + 1]
        dk_ref[:, cols] = joined(a, turned(b)).astype(BF)
        dv_ref[:, cols] = joined(turned(a), b).astype(BF)


def grads_call(row, near, tokens, features):
    return pl.pallas_call(
        grads_kernel,
        in_specs=any_specs(2),
        out_shape=[jax.ShapeDtypeStruct((tokens, features), BF)] * 3,
        scratch_shapes=[
            pltpu.VMEM((ROW, tokens, LANES), BF),
            pltpu.VMEM((ROW, tokens // 2, LANES), BF),
            pltpu.SemaphoreType.DMA((2,)),
        ],
        compiler_params=pltpu.CompilerParams(vmem_limit_bytes=16 << 20),
    )(row, near)


def final_kernel(parts_in, dpos_ref, dw_ref, parts_ref, sems):
    brought([(parts_in, parts_ref)], sems)
    cut = dpos_ref.shape[0]
    total = parts_ref[0].astype(F32)
    for z in range(1, parts_ref.shape[0]):
        total = total + parts_ref[z].astype(F32)
    dpos_ref[...] = total[:cut].astype(BF)
    dw_ref[...] = total[cut:].astype(BF)


def final_call(parts, pos_rows):
    rows, features = parts.shape[1:]
    shapes = [(pos_rows, features), (rows - pos_rows, features)]
    return pl.pallas_call(
        final_kernel,
        in_specs=any_specs(1),
        out_shape=[jax.ShapeDtypeStruct(shape, BF) for shape in shapes],
        scratch_shapes=[pltpu.VMEM(parts.shape, BF), pltpu.SemaphoreType.DMA((1,))],
        compiler_params=pltpu.CompilerParams(vmem_limit_bytes=16 << 20),
    )(parts)


def shifted(block, distance):
    count = lax.axis_size("ctx")
    return lax.ppermute(block, "ctx", [(i, (i + distance) % count) for i in range(count)])


def swapped(block, bit):
    return lax.ppermute(block, "head", [(i, i ^ bit) for i in range(lax.axis_size("head"))])


def in_row(block):
    count = lax.axis_size("ctx")
    groups = [list(range(r, r + ROW)) for r in range(0, count, ROW)]
    return lax.all_to_all(block, "ctx", 0, 0, axis_index_groups=groups)


def in_column(block):
    count = lax.axis_size("ctx")
    groups = [list(range(x, count, ROW)) for x in range(ROW)]
    return lax.all_to_all(block, "ctx", 0, 0, axis_index_groups=groups)


def masked(block, mask):
    return lax.ppermute(block, "ctx", [(i, i ^ mask) for i in range(lax.axis_size("ctx"))])


def body(
    query, key, value, pos_store, owner, block_mask, content_bias, pos_bias, out_weight, d_layer
):
    tokens, features = query.shape
    slot_count = owner.shape[0]
    slot_rows = pos_store.shape[0]
    column = slot_count // ROW
    across = swapped(d_layer, 2)
    far_pos = [pos_store] + [masked(pos_store, ROW * 4 * j) for j in range(1, 4)]
    packed = pack_call(block_mask, query, key, value)
    packed, across, *far_pos = lax.optimization_barrier((packed, across, *far_pos))
    far_pos = jnp.concatenate(far_pos, axis=0)
    slots = [far_pos] + [masked(far_pos, ROW * j) for j in range(1, 4)]
    row = in_row(packed)
    halo = shifted(row[1:, :tokens], ROW)
    grads = [d_layer, swapped(d_layer, 1), across, swapped(across, 1)]
    ga = in_row(mix_call(grads, out_weight, slots))
    near, own, far = core_call(owner, row, halo, ga, content_bias[None], pos_bias[None])
    back = shifted(far, -ROW)
    near = in_row(near)
    near, back = lax.optimization_barrier((near, back))
    met = in_row(weight_call(near, grads, own, back))
    parts = in_column(sum_call(met, near, column, slot_rows, features, tokens))
    grad_query, grad_key, grad_value = grads_call(met, near, tokens, features)
    grad_pos, grad_weight = final_call(parts, slot_rows)
    return grad_query, grad_key, grad_value, grad_pos, grad_weight.T


def solution(mesh):
    spread = P("ctx", "head")
    return jax.shard_map(
        body,
        mesh=mesh,
        in_specs=(
            spread, spread, spread, spread, P(), P("ctx", None), P("head"), P("head"),
            P("head", None), spread,
        ),
        out_specs=(spread, spread, spread, spread, P("head", "ctx")),
        check_vma=False,
    )
```

```python
import functools

import jax
import jax.numpy as jnp
from jax import lax
from jax.experimental import pallas as pl
from jax.experimental.pallas import tpu as pltpu
from jax.sharding import PartitionSpec as P

HD = 64
LANES = 128
NEG = -1e30
ROW = 4
BF = jnp.bfloat16
F32 = jnp.float32


def nt(a, b):
    return lax.dot_general(a, b, (((1,), (1,)), ((), ())), preferred_element_type=F32)


def nn(a, b):
    return lax.dot_general(a, b, (((1,), (0,)), ((), ())), preferred_element_type=F32)


def tn(a, b):
    return lax.dot_general(a, b, (((0,), (0,)), ((), ())), preferred_element_type=F32)


def lanes():
    return lax.broadcasted_iota(jnp.int32, (1, LANES), 1)


def turned(block, shift=HD):
    return pltpu.roll(block.astype(F32), shift, 1)


def joined(low, high):
    return jnp.where(lanes() < HD, low.astype(F32), high.astype(F32))


def of_head(array, head):
    pair = array[:, head // 2 * LANES : (head // 2 + 1) * LANES]
    return turned(pair) if head % 2 else pair.astype(F32)


def halves(array, head):
    both = of_head(array, head)
    middle = both.shape[0] // 2
    return joined(both[:middle], turned(both[middle:]))


def whole_of(first, second):
    top = joined(first, turned(second))
    bottom = joined(turned(first), second)
    return jnp.concatenate([top, bottom], axis=0)


def anti_diagonal(size):
    row = lax.broadcasted_iota(jnp.int32, (size, size), 0)
    col = lax.broadcasted_iota(jnp.int32, (size, size), 1)
    return (row + col == size - 1).astype(F32).astype(BF)


def vmem_specs(count):
    return [pl.BlockSpec(memory_space=pltpu.VMEM)] * count


def smem_specs(count):
    return [pl.BlockSpec(memory_space=pltpu.SMEM)] * count


def any_specs(count):
    return [pl.BlockSpec(memory_space=pl.ANY)] * count


def hbm_specs(count):
    return [pl.BlockSpec(memory_space=pltpu.HBM)] * count


def whole_spec(shape):
    return pl.BlockSpec(shape, lambda *_: (0,) * len(shape))


def brought(pairs, sems, meanwhile=lambda: None):
    copies = [
        pltpu.make_async_copy(source, target, sems.at[i])
        for i, (source, target) in enumerate(pairs)
    ]
    for copy in copies:
        copy.start()
    meanwhile()
    for copy in copies:
        copy.wait()


def pack_kernel(mask_ref, q_in, k_in, v_in, out_ref, q_ref, k_ref, v_ref, sems):
    brought([(q_in, q_ref), (k_in, k_ref), (v_in, v_ref)], sems)
    tokens = q_ref.shape[0]
    half = tokens // 2
    flags = jnp.zeros((16, LANES), F32)
    for lag in range(mask_ref.shape[1]):
        flags = jnp.where(lanes() == lag, mask_ref[0, lag].astype(F32), flags)
    for h in range(ROW):
        out_ref[h, :tokens, :] = joined(of_head(k_ref, h), turned(of_head(v_ref, h))).astype(BF)
        out_ref[h, tokens : tokens + half, :] = halves(q_ref, h).astype(BF)
        out_ref[h, tokens + half :, :] = flags.astype(BF)


def pack_call(mask, q, k, v):
    tokens = q.shape[0]
    rows = tokens + tokens // 2 + 16
    return pl.pallas_call(
        pack_kernel,
        in_specs=smem_specs(1) + hbm_specs(3),
        out_shape=pltpu.HBM((ROW, rows, LANES), BF),
        scratch_shapes=[pltpu.VMEM(a.shape, BF) for a in (q, k, v)]
        + [pltpu.SemaphoreType.DMA((3,))],
        compiler_params=pltpu.CompilerParams(vmem_limit_bytes=60 << 20),
    )(mask, q, k, v)


def mix_kernel(
    g0_in, g1_in, g2_in, g3_in, weight_in, s0_in, s1_in, s2_in, s3_in, out_ref,
    g0, g1, g2, g3, weight_ref, pos_ref, sems,
):
    rows = s0_in.shape[0]
    pairs = [(g0_in, g0), (g1_in, g1), (g2_in, g2), (g3_in, g3), (weight_in, weight_ref)]
    for i, part in enumerate((s0_in, s1_in, s2_in, s3_in)):
        pairs.append((part, pos_ref.at[i * rows : (i + 1) * rows]))
    brought(pairs, sems)
    tokens, features = g0.shape
    mixed = None
    for b, grad in enumerate((g0, g1, g2, g3)):
        at = pl.multiple_of((lax.axis_index("head") ^ b) * features, features)
        part = nt(grad[...], weight_ref[:, pl.ds(at, features)])
        mixed = part if mixed is None else mixed + part
    mixed = mixed.astype(BF)
    for h in range(ROW):
        out_ref[h, : tokens // 2, :] = halves(mixed, h).astype(BF)
        out_ref[h, tokens // 2 :, :] = halves(pos_ref, h).astype(BF)


def mix_call(grads, out_weight, slots):
    tokens, features = grads[0].shape
    rows = 4 * slots[0].shape[0]
    return pl.pallas_call(
        mix_kernel,
        in_specs=any_specs(9),
        out_shape=pltpu.HBM((ROW, (tokens + rows) // 2, LANES), BF),
        scratch_shapes=[pltpu.VMEM(a.shape, BF) for a in (*grads, out_weight)]
        + [pltpu.VMEM((rows, features), BF), pltpu.SemaphoreType.DMA((9,))],
        compiler_params=pltpu.CompilerParams(vmem_limit_bytes=16 << 20),
    )(*grads, out_weight, *slots)


def key_pairs(row_in, halo_in, keys, query, tokens):
    pairs = [(halo_in.at[b], keys.at[b * tokens : (b + 1) * tokens]) for b in range(ROW - 1)]
    for b in range(ROW):
        at = (ROW - 1 + b) * tokens
        pairs.append((row_in.at[b, 0:tokens], keys.at[at : at + tokens]))
        pairs.append((row_in.at[b, tokens : tokens + tokens // 2], query.at[b]))
    return pairs


def core_kernel(
    owner_ref, row_in, halo_in, ga_in, cb_in, pb_in,
    near_ref, own_ref, far_ref,
    keys, queries, pos_ref, ga_ref, dist_out, table, flipped, grads, dist,
    score_ref, rel_ref, low_ref, ds_ref, spread_ref, dot_ref, flag_ref, cb_ref, pb_ref, sems,
):
    tokens = halo_in.shape[1]
    half = tokens // 2
    span = ROW * tokens
    wide = span + half
    block = pl.program_id(0)
    anti = anti_diagonal(half)

    @pl.when(block == 0)
    def _():
        pairs = key_pairs(row_in, halo_in, keys, queries, tokens)
        count = owner_ref.shape[0]
        packed = pos_ref.shape[2]
        rows = 2 * packed * ROW // count
        pairs += [(ga_in.at[:, 0:half], ga_ref), (ga_in.at[:, half : half + packed], pos_ref.at[0])]
        pairs.append((row_in.at[:, tokens + half : tokens + half + 16], flag_ref))

        def clear():
            grads[...] = jnp.zeros_like(grads)
            dist[...] = jnp.zeros_like(dist)
            table[0:tokens, :] = jnp.zeros((tokens, LANES), BF)

        brought(pairs, sems, clear)
        for b in range(ROW):
            pos_ref[1, b] = turned(pos_ref[0, b]).astype(BF)
        turn = (ROW - (lax.axis_index("ctx") & 3)) * HD % cb_in.shape[1]
        for bias_in, bias_ref in ((cb_in, cb_ref), (pb_in, pb_ref)):
            bias = jnp.broadcast_to(bias_in[...], (8, bias_in.shape[1]))
            bias_ref[...] = pltpu.roll(bias, turn, 1)[0:1, :LANES]
        for d in range(count):
            slot = owner_ref[d]
            apart = (slot >> 2) ^ (lax.axis_index("ctx") >> 2)
            place = (apart & 3) * 4 + (apart >> 2)
            at = pl.multiple_of((place & 7) * rows, rows)
            both = pos_ref[place >> 3, slot & 3, pl.ds(at, rows), :]
            table[tokens + d * rows : tokens + (d + 1) * rows, :] = both
        parts = (tokens + span) // half
        for i in range(parts):
            flipped[(parts - 1 - i) * half : (parts - i) * half, :] = nn(
                anti, table[i * half : (i + 1) * half, :]
            ).astype(BF)

    lane = lanes()
    low = lane < HD
    scale = jnp.asarray(0.125, BF)
    starts = [pl.multiple_of((block + w) * tokens, tokens) for w in range(ROW)]
    kept = []
    dqs = []
    chunk = 16
    groups = [slice(c, c + chunk) for c in range(0, half, chunk)]
    barred = []
    for lag in range(ROW - 1, 0, -1):
        there = (lax.axis_index("ctx") & ~3) + block >= lag
        flag = flag_ref[block, 0:1, lag : lag + 1].astype(F32)
        barred.append(jnp.where(there & (flag > 0.5), 0.0, NEG))
    state = [{}, {}]

    def cols_of(w, r):
        width = half if r == 0 and w == ROW - 1 else tokens
        return width, slice(w * tokens, w * tokens + width)

    def first(r):
        query = queries[block].astype(F32)
        ga = ga_ref[block].astype(F32)
        query = turned(query) if r == 1 else query
        ga = turned(ga) if r == 0 else ga
        ga = jnp.where(low, 0.0, ga)
        cq = jnp.where(low, query + cb_ref[...], 0.0).astype(BF)
        pq = jnp.where(low, query + pb_ref[...], 0.0).astype(BF)
        state[r].update(ga=ga, gal=ga.astype(BF), cq=cq, pq=pq)
        base = half * (1 - r)
        width = span if r == 0 else wide
        rel_ref[r, :, :width] = nt(pq * scale, flipped[base : base + width, :])
        cqs = cq * scale
        for w in range(ROW):
            width, cols = cols_of(w, r)
            score_ref[r, :, cols] = nt(cqs, keys[pl.ds(starts[w], width), :])

    def soften(r):
        for g in groups:
            moved = pltpu.roll(
                rel_ref[r, g, :], (span + 1 + g.start) % wide, 1, stride=1, stride_axis=0
            )
            scores = []
            for w in range(ROW):
                width, cols = cols_of(w, r)
                s = score_ref[r, g, cols] + moved[:, cols]
                if w == ROW - 1:
                    row = lax.broadcasted_iota(jnp.int32, (chunk, width), 0) + r * half + g.start
                    col = lax.broadcasted_iota(jnp.int32, (chunk, width), 1)
                    s = jnp.where(col <= row, s, NEG)
                else:
                    s = s + barred[w]
                scores.append(s)
            parts = [s[:, x : x + half] for s in scores for x in range(0, s.shape[1], half)]
            top = functools.reduce(jnp.maximum, parts)
            top = jnp.max(top, axis=1, keepdims=True)
            weights = [jnp.exp(s - top) for s in scores]
            parts = [e[:, x : x + half] for e in weights for x in range(0, e.shape[1], half)]
            total = functools.reduce(jnp.add, parts)
            inv = 1.0 / jnp.sum(total, axis=1, keepdims=True)
            for w in range(ROW):
                _, cols = cols_of(w, r)
                p = weights[w] * inv
                score_ref[r, g, cols] = p
                low_ref[r, g, cols] = p.astype(BF)

    def second(r):
        att = None
        for w in range(ROW):
            width, cols = cols_of(w, r)
            part = nn(low_ref[r, :, cols], keys[pl.ds(starts[w], width), :])
            att = part if att is None else att + part
        att = att.astype(BF).astype(F32)
        state[r]["att"] = turned(att) if r == 0 else att
        dot = jnp.sum(state[r]["ga"] * att, axis=1, keepdims=True)
        dot_ref[r] = jnp.broadcast_to(dot, (half, LANES))
        for w in range(ROW):
            width, cols = cols_of(w, r)
            rel_ref[r, :, cols] = nt(state[r]["gal"], keys[pl.ds(starts[w], width), :])

    def steepen(r):
        for g in groups:
            dot = dot_ref[r, g, 0:1]
            for w in range(ROW):
                _, cols = cols_of(w, r)
                ds = 0.125 * score_ref[r, g, cols] * (rel_ref[r, g, cols] - dot)
                ds_ref[r, g, cols] = ds.astype(BF)

    def third(r):
        acc = None
        for w in range(ROW):
            width, cols = cols_of(w, r)
            ds = ds_ref[r, :, cols]
            for x in range(width // half):
                at = (2 * ROW - 1 - (2 * w + x)) * half
                rel_ref[r, :, at : at + half] = nn(ds[:, x * half : (x + 1) * half], anti)
        if r == 0:
            rel_ref[r, :, :half] = jnp.zeros((half, half), F32)
        rel_ref[r, :, span:] = jnp.zeros((half, wide - span), F32)
        for w in range(ROW):
            width, cols = cols_of(w, r)
            ds = ds_ref[r, :, cols]
            grads[:, pl.ds(starts[w], width)] += tn(state[r]["cq"], ds) + tn(
                state[r]["gal"], low_ref[r, :, cols]
            )
            part = nn(ds, keys[pl.ds(starts[w], width), :])
            acc = part if acc is None else acc + part
        state[r]["acc"] = acc

    def slant(r):
        for g in groups:
            spread_ref[r, g, :] = pltpu.roll(
                rel_ref[r, g, :], 1 + g.start, 1, stride=1, stride_axis=0
            ).astype(BF)

    def fourth(r):
        skip = half if r == 0 else 0
        start, stop = half * r + skip, half * r + wide
        spread = spread_ref[r, :, skip:]
        acc = state[r]["acc"] + nn(spread, table[start:stop, :])
        dist[:, start:stop] += tn(state[r]["pq"], spread)
        state[r]["acc"] = turned(acc) if r == 1 else acc

    first(0)
    for stage, other in (
        (soften, first), (second, soften), (steepen, second), (third, steepen), (slant, third),
        (fourth, slant),
    ):
        stage(0)
        other(1)
    fourth(1)
    kept = [part["att"] for part in state]
    dqs = [part["acc"] for part in state]
    near_ref[block, :half, :] = joined(kept[0], kept[1]).astype(BF)
    near_ref[block, half:tokens, :] = joined(dqs[0], dqs[1]).astype(BF)

    @pl.when(block == ROW - 1)
    def _():
        for b in range(ROW - 1):
            far_ref[b] = grads[:, b * tokens : (b + 1) * tokens].T.astype(BF)
        for b in range(ROW):
            at = (ROW - 1 + b) * tokens
            own_ref[b] = grads[:, at : at + tokens].T
        count = owner_ref.shape[0]
        packed = pos_ref.shape[2]
        rows = 2 * packed * ROW // count
        dist_out[...] = dist[:, tokens:].T
        for d in range(count):
            slot = owner_ref[d]
            part = dist_out[d * rows : (d + 1) * rows, :].astype(BF)
            place = slot >> 2
            at = pl.multiple_of((place & 7) * rows, rows)
            pos_ref[place >> 3, slot & 3, pl.ds(at, rows), :] = part
        for b in range(ROW):
            near_ref[b, tokens:, :] = joined(pos_ref[0, b], turned(pos_ref[1, b])).astype(BF)


def core_call(owner, row, halo, ga, cb, pb):
    tokens = halo.shape[1]
    half = tokens // 2
    packed = ga.shape[1] - half
    rel = ROW * packed * 2
    shapes = [
        ((ROW, tokens + packed, LANES), BF), ((ROW, tokens, LANES), F32),
        ((ROW - 1, tokens, LANES), BF),
    ]
    return pl.pallas_call(
        core_kernel,
        grid=(ROW,),
        in_specs=smem_specs(1) + any_specs(3) + vmem_specs(2),
        out_specs=[whole_spec(shape) for shape, _ in shapes],
        out_shape=[pltpu.HBM(shape, dtype) for shape, dtype in shapes],
        scratch_shapes=[
            pltpu.VMEM(((2 * ROW - 1) * tokens, LANES), BF),
            pltpu.VMEM((ROW, half, LANES), BF),
            pltpu.VMEM((2, ROW, packed, LANES), BF),
            pltpu.VMEM((ROW, half, LANES), BF),
            pltpu.VMEM((rel, LANES), F32),
            pltpu.VMEM((tokens + rel, LANES), BF),
            pltpu.VMEM((tokens + rel, LANES), BF),
            pltpu.VMEM((LANES, (2 * ROW - 1) * tokens), F32),
            pltpu.VMEM((LANES, tokens + rel), F32),
            pltpu.VMEM((2, half, ROW * tokens), F32),
            pltpu.VMEM((2, half, ROW * tokens + half), F32),
            pltpu.VMEM((2, half, ROW * tokens), BF),
            pltpu.VMEM((2, half, ROW * tokens), BF),
            pltpu.VMEM((2, half, ROW * tokens + half), BF),
            pltpu.VMEM((2, half, LANES), F32),
            pltpu.VMEM((ROW, 16, LANES), BF),
            pltpu.VMEM((1, LANES), F32),
            pltpu.VMEM((1, LANES), F32),
            pltpu.SemaphoreType.DMA((3 * ROW + 2,)),
        ],
        compiler_params=pltpu.CompilerParams(vmem_limit_bytes=60 << 20),
        cost_estimate=pl.CostEstimate(
            flops=40_000_000_000, bytes_accessed=8_000_000, transcendentals=0
        ),
    )(owner, row, halo, ga, cb, pb)


def weight_kernel(
    att_in, g0_in, g1_in, g2_in, g3_in, own_in, far_in, out_ref,
    att_ref, g0, g1, g2, g3, own_ref, far_ref, sems,
):
    half = att_ref.shape[1]
    tokens, features = g0.shape
    sources = [att_in.at[:, 0:half], g0_in, g1_in, g2_in, g3_in, own_in, far_in]
    brought(zip(sources, [att_ref, g0, g1, g2, g3, own_ref, far_ref]), sems)
    for b in range(ROW):
        grad = own_ref[b]
        if b > 0:
            grad = grad + far_ref[b - 1].astype(F32)
        out_ref[b, :tokens, :] = grad.astype(BF)
    rows = 16
    chunks = features // rows
    column = 4 * features // (ROW * rows)
    for pair in range(features // LANES):
        att = whole_of(att_ref[2 * pair], att_ref[2 * pair + 1]).astype(BF)
        for b, grad in enumerate((g0, g1, g2, g3)):
            term = tn(att, grad[...]).T.astype(BF)
            first = (lax.axis_index("head") ^ b) * (chunks // ROW)
            for c in range(chunks):
                at = tokens + (pair * column + first + c // ROW) * rows
                out_ref[c % ROW, pl.ds(pl.multiple_of(at, rows), rows), :] = term[
                    c * rows : (c + 1) * rows
                ]


def weight_call(near, grads, own, far):
    tokens, features = grads[0].shape
    rows = tokens + 4 * features // ROW * (features // LANES)
    return pl.pallas_call(
        weight_kernel,
        in_specs=any_specs(7),
        out_shape=pltpu.HBM((ROW, rows, LANES), BF),
        scratch_shapes=[pltpu.VMEM((ROW, tokens // 2, LANES), BF)]
        + [pltpu.VMEM(a.shape, a.dtype) for a in (*grads, own, far)]
        + [pltpu.SemaphoreType.DMA((7,))],
        compiler_params=pltpu.CompilerParams(vmem_limit_bytes=16 << 20),
    )(near, *grads, own, far)


def sum_kernel(row_in, near_in, out_ref, row_ref, near_ref, sems):
    column, rows, features = out_ref.shape
    weight_rows = 16
    pos_rows = rows - weight_rows
    tokens = row_in.shape[1] - column * weight_rows * (features // LANES)
    near_rows = near_in.shape[1]
    sources = [row_in.at[:, tokens:], near_in.at[:, tokens:near_rows]]
    brought(zip(sources, [row_ref, near_ref]), sems)
    for pair in range(features // LANES):
        cols = slice(pair * LANES, (pair + 1) * LANES)
        pos = whole_of(near_ref[2 * pair], near_ref[2 * pair + 1]).astype(BF)
        part = slice(pair * column * weight_rows, (pair + 1) * column * weight_rows)
        total = row_ref[0, part, :].astype(F32)
        for x in range(1, ROW):
            total = total + row_ref[x, part, :].astype(F32)
        total = total.astype(BF)
        for z in range(column):
            out_ref[z, :pos_rows, cols] = pos[z * pos_rows : (z + 1) * pos_rows]
            out_ref[z, pos_rows:, cols] = total[z * weight_rows : (z + 1) * weight_rows]


def sum_call(row, near, column, pos_rows, features, tokens):
    return pl.pallas_call(
        sum_kernel,
        in_specs=any_specs(2),
        out_shape=pltpu.HBM((column, pos_rows + 16, features), BF),
        scratch_shapes=[
            pltpu.VMEM((ROW, row.shape[1] - tokens, LANES), BF),
            pltpu.VMEM((ROW, near.shape[1] - tokens, LANES), BF),
            pltpu.SemaphoreType.DMA((2,)),
        ],
        compiler_params=pltpu.CompilerParams(vmem_limit_bytes=16 << 20),
    )(row, near)


def grads_kernel(row_in, near_in, dq_ref, dk_ref, dv_ref, row_ref, near_ref, sems):
    tokens = dq_ref.shape[0]
    sources = [row_in.at[:, 0:tokens], near_in.at[:, tokens // 2 : tokens]]
    brought(zip(sources, [row_ref, near_ref]), sems)
    for pair in range(ROW // 2):
        cols = slice(pair * LANES, (pair + 1) * LANES)
        dq_ref[:, cols] = whole_of(near_ref[2 * pair], near_ref[2 * pair + 1]).astype(BF)
        a, b = row_ref[2 * pair], row_ref[2 * pair + 1]
        dk_ref[:, cols] = joined(a, turned(b)).astype(BF)
        dv_ref[:, cols] = joined(turned(a), b).astype(BF)


def grads_call(row, near, tokens, features):
    return pl.pallas_call(
        grads_kernel,
        in_specs=any_specs(2),
        out_shape=[jax.ShapeDtypeStruct((tokens, features), BF)] * 3,
        scratch_shapes=[
            pltpu.VMEM((ROW, tokens, LANES), BF),
            pltpu.VMEM((ROW, tokens // 2, LANES), BF),
            pltpu.SemaphoreType.DMA((2,)),
        ],
        compiler_params=pltpu.CompilerParams(vmem_limit_bytes=16 << 20),
    )(row, near)


def final_kernel(parts_in, dpos_ref, dw_ref, parts_ref, sems):
    brought([(parts_in, parts_ref)], sems)
    cut = dpos_ref.shape[0]
    total = parts_ref[0].astype(F32)
    for z in range(1, parts_ref.shape[0]):
        total = total + parts_ref[z].astype(F32)
    dpos_ref[...] = total[:cut].astype(BF)
    dw_ref[...] = total[cut:].astype(BF)


def final_call(parts, pos_rows):
    rows, features = parts.shape[1:]
    shapes = [(pos_rows, features), (rows - pos_rows, features)]
    return pl.pallas_call(
        final_kernel,
        in_specs=any_specs(1),
        out_shape=[jax.ShapeDtypeStruct(shape, BF) for shape in shapes],
        scratch_shapes=[pltpu.VMEM(parts.shape, BF), pltpu.SemaphoreType.DMA((1,))],
        compiler_params=pltpu.CompilerParams(vmem_limit_bytes=16 << 20),
    )(parts)


def shifted(block, distance):
    count = lax.axis_size("ctx")
    return lax.ppermute(block, "ctx", [(i, (i + distance) % count) for i in range(count)])


def swapped(block, bit):
    return lax.ppermute(block, "head", [(i, i ^ bit) for i in range(lax.axis_size("head"))])


def in_row(block):
    count = lax.axis_size("ctx")
    groups = [list(range(r, r + ROW)) for r in range(0, count, ROW)]
    return lax.all_to_all(block, "ctx", 0, 0, axis_index_groups=groups)


def in_column(block):
    count = lax.axis_size("ctx")
    groups = [list(range(x, count, ROW)) for x in range(ROW)]
    return lax.all_to_all(block, "ctx", 0, 0, axis_index_groups=groups)


def masked(block, mask):
    return lax.ppermute(block, "ctx", [(i, i ^ mask) for i in range(lax.axis_size("ctx"))])


def body(
    query, key, value, pos_store, owner, block_mask, content_bias, pos_bias, out_weight, d_layer
):
    tokens, features = query.shape
    slot_count = owner.shape[0]
    slot_rows = pos_store.shape[0]
    column = slot_count // ROW
    across = swapped(d_layer, 2)
    far_pos = [pos_store] + [masked(pos_store, ROW * 4 * j) for j in range(1, 4)]
    packed = pack_call(block_mask, query, key, value)
    packed, across = lax.optimization_barrier((packed, across))
    far_pos = jnp.concatenate(far_pos, axis=0)
    slots = [far_pos] + [masked(far_pos, ROW * j) for j in range(1, 4)]
    row = in_row(packed)
    halo = shifted(row[1:, :tokens], ROW)
    grads = [d_layer, swapped(d_layer, 1), across, swapped(across, 1)]
    ga = in_row(mix_call(grads, out_weight, slots))
    near, own, far = core_call(owner, row, halo, ga, content_bias[None], pos_bias[None])
    back = shifted(far, -ROW)
    near = in_row(near)
    near, back = lax.optimization_barrier((near, back))
    met = in_row(weight_call(near, grads, own, back))
    parts = in_column(sum_call(met, near, column, slot_rows, features, tokens))
    grad_query, grad_key, grad_value = grads_call(met, near, tokens, features)
    grad_pos, grad_weight = final_call(parts, slot_rows)
    return grad_query, grad_key, grad_value, grad_pos, grad_weight.T


def solution(mesh):
    spread = P("ctx", "head")
    return jax.shard_map(
        body,
        mesh=mesh,
        in_specs=(
            spread, spread, spread, spread, P(), P("ctx", None), P("head"), P("head"),
            P("head", None), spread,
        ),
        out_specs=(spread, spread, spread, spread, P("head", "ctx")),
        check_vma=False,
    )
```
